32 devices in a mesh: seq: 8 (over y, x, core), fsdp: 4 (over z).
Axes of the slice: x: 2, y: 2, z: 4, core: 2. Of those that a mesh axis runs over, the one named last changes fastest.
Arguments:
- clean_states: bfloat16 [4, 2048, 4096], P('fsdp', 'seq'), may hold values from -6 to 6
- noise_mask: int32 [4, 2048], P('fsdp', 'seq'), may hold values from 0 to 1, as said below
- mask_embed: bfloat16 [4096], replicated, may hold values from -6 to 6
- queries: bfloat16 [4, 2048, 2048], P('fsdp', 'seq'), may hold values from -96 to 96
- w_key: bfloat16 [4096, 512], P('fsdp'), may hold values from -0.09375 to 0.09375
- w_value: bfloat16 [4096, 512], P('fsdp'), may hold values from -0.09375 to 0.09375
Outputs:
- noisy_attention: bfloat16 [4, 2048, 2048], P('fsdp', 'seq')
The draws below stay inside these ranges and needn't reach their ends.
Inputs may be any that keep to these rules, and one draw needn't show every extreme that they name: `noise_mask`: each block of 256 positions has its own masking rate; 1 marks a masked position.
All inputs are finite; a program needn't handle non-finite values.
Results may differ from the reference program's by a relative error of at most 0.011.
Values may be sent and summed in bfloat16 or wider, within the bound.
No kernel may reach another device: no remote copies, remote signals or barrier semaphores. Data moves between devices by JAX's collectives and lax.ppermute only.
A program may use at most 64 MiB of HBM per device.

```python
import jax
import jax.numpy as jnp
from jax import lax

D = 4096
HEADS = 16
KV_HEADS = 4
HEAD_DIM = 128
BLOCK = 256
LEN = 2048
SEQS = 4


def draw_noise_mask(key, part):
    key_levels, key_ticks = jax.random.split(jax.random.fold_in(key, 11))
    levels = jax.random.randint(key_levels, (SEQS, LEN // BLOCK, 1), 0, 65)
    ticks = jax.random.randint(key_ticks, (SEQS, LEN // BLOCK, BLOCK), 0, 64)
    return (ticks < levels).astype(jnp.int32).reshape(SEQS, LEN)


def draw_queries(key, part):
    key_base = jax.random.fold_in(jax.random.fold_in(key, 23), 0)
    shape = (SEQS, LEN, HEADS * HEAD_DIM)
    return jnp.clip(jax.random.normal(key_base, shape, jnp.float32) * 3.0, -18.0, 18.0).astype(jnp.bfloat16)


def steps_of(stream_key, extent, cuts, low, top_value):
    gain, own = 1.0, jax.random.fold_in(stream_key, 6)
    for position, shards_of in cuts:
        heights = jnp.exp(jax.random.uniform(jax.random.fold_in(own, position), (shards_of,), jnp.float32, low / len(cuts), top_value / len(cuts)))
        gain = gain * jnp.repeat(heights, extent[position] // shards_of).reshape([-1 if axis == position else 1 for axis in range(len(extent))])
    return gain


def gaussian(rng, extent, deviation, limit, cuts=(), kind=jnp.bfloat16):
    entries = deviation * jax.random.normal(rng, extent, jnp.float32)
    if cuts:
        entries = entries * steps_of(rng, extent, cuts, -0.22, 0.18)
    return jnp.clip(entries, -limit, limit).astype(kind)


def setup_inputs(seed: int = 0) -> dict:
    key_list = jax.random.split(jax.random.key(seed), 7)
    return {
        "clean_states": gaussian(key_list[0], (SEQS, LEN, D), 1.0, 6.0, ((0, 4), (1, 8))),
        "noise_mask": draw_noise_mask(jax.random.fold_in(key_list[6], 71), 0),
        "mask_embed": gaussian(key_list[2], (D,), 1.0, 6.0),
        "queries": draw_queries(jax.random.fold_in(key_list[6], 71), 0),
        "w_key": gaussian(key_list[4], (D, KV_HEADS * HEAD_DIM), D ** -0.5, 0.09375, ((0, 4),)),
        "w_value": gaussian(key_list[5], (D, KV_HEADS * HEAD_DIM), D ** -0.5, 0.09375, ((0, 4),)),
    }


ROPE_BASE = 500000.0


def rotate(key_rows, positions):
    half_dim = key_rows.shape[-1] // 2
    frequency = ROPE_BASE ** (-(jnp.arange(half_dim, dtype=jnp.float32) * 2.0 / key_rows.shape[-1]))
    angles = positions[:, None] * frequency[None, :]
    cosine = jnp.cos(angles)[:, None, :]
    sine_part = jnp.sin(angles)[:, None, :]
    first_half = key_rows[..., :half_dim]
    second_half = key_rows[..., half_dim:]
    return jnp.concatenate([first_half * cosine - second_half * sine_part, second_half * cosine + first_half * sine_part], -1)


def reference(clean_states, noise_mask, mask_embed, queries, w_key, w_value):
    length = clean_states.shape[1]
    kv_width = w_key.shape[1]
    kv_count = kv_width // HEAD_DIM
    groups = HEADS // kv_count
    blocks = length // BLOCK
    positions = jnp.arange(length, dtype=jnp.int32)
    score_scale = HEAD_DIM ** -0.5

    def one_sequence(inputs):
        states, noise_marks, query_rows = inputs
        noisy_rows = jnp.where(noise_marks[:, None] == 1, mask_embed[None, :], states)
        both_rows = jnp.concatenate([states, noisy_rows], 0)
        key_sums = jnp.dot(both_rows, w_key, preferred_element_type=jnp.float32).reshape(2 * length, kv_count, HEAD_DIM)
        both_positions = jnp.concatenate([positions, positions]).astype(jnp.float32)
        key_rows = rotate(key_sums, both_positions).astype(jnp.bfloat16)
        value_rows = jnp.dot(both_rows, w_value, preferred_element_type=jnp.float32).astype(jnp.bfloat16).reshape(2 * length, kv_count, HEAD_DIM)
        key_rows, value_rows = lax.optimization_barrier((key_rows, value_rows))
        clean_keys = key_rows[:length].astype(jnp.float32)
        clean_values = value_rows[:length].astype(jnp.float32)
        noisy_keys = key_rows[length:].reshape(blocks, BLOCK, kv_count, HEAD_DIM)
        noisy_values = value_rows[length:].reshape(blocks, BLOCK, kv_count, HEAD_DIM)
        query_blocks = query_rows.reshape(blocks, BLOCK, kv_count, groups, HEAD_DIM)

        def one_block(inner):
            block_index, block_queries, own_keys, own_values = inner
            all_keys = jnp.concatenate([clean_keys, own_keys.astype(jnp.float32)], 0)
            all_values = jnp.concatenate([clean_values, own_values.astype(jnp.float32)], 0)
            scores = jnp.einsum('qkgd,tkd->qkgt', block_queries.astype(jnp.float32), all_keys) * score_scale
            allowed = jnp.concatenate([positions // BLOCK < block_index, jnp.ones((BLOCK,), bool)])
            scores = jnp.where(allowed[None, None, None, :], scores, -1e30)
            row_max = jnp.max(scores, -1, keepdims=True)
            probs = jnp.where(allowed[None, None, None, :], jnp.exp(scores - row_max), 0.0)
            row_total = jnp.sum(probs, -1)
            rounded = lax.optimization_barrier(probs.astype(jnp.bfloat16))
            mixture = jnp.einsum('qkgt,tkd->qkgd', rounded.astype(jnp.float32), all_values)
            return (mixture / row_total[..., None]).astype(jnp.bfloat16).reshape(BLOCK, kv_count * groups * HEAD_DIM)

        outputs = lax.map(one_block, (jnp.arange(blocks, dtype=jnp.int32), query_blocks, noisy_keys, noisy_values))
        return outputs.reshape(length, kv_count * groups * HEAD_DIM)

    return lax.map(one_sequence, (clean_states, noise_mask, queries))
```

```python
import functools
import math

import jax
import jax.numpy as jnp
from jax import lax
from jax.experimental import pallas as pl
from jax.experimental.pallas import tpu as pltpu
from jax.sharding import PartitionSpec as P

HEADS = 16
HEAD_DIM = 128
BLOCK = 256
ROPE_BASE = 500000.0
MASK_ROWS = 16
LOG2E = math.log2(math.e)
VMEM_LIMIT = 48 * 1024 * 1024


def rotation(positions):
    half_dim = HEAD_DIM // 2
    frequency = ROPE_BASE ** (-(jnp.arange(half_dim, dtype=jnp.float32) * 2.0 / HEAD_DIM))
    angles = positions.astype(jnp.float32)[:, None] * frequency[None, :]
    cosine = jnp.cos(angles)
    sine = jnp.sin(angles)
    return jnp.concatenate([cosine, cosine], -1), jnp.concatenate([-sine, sine], -1)


def partial_kernel(count, has_total, starts, rows_ref, *refs):
    total_in = refs[0] if has_total else None
    pieces = refs[int(has_total) : int(has_total) + count]
    total_out = refs[-1]
    total_out[...] = gather_sum(starts, rows_ref, total_in, pieces)


def gather_sum(starts, rows_ref, total_in, pieces):
    total = None if total_in is None else total_in[...]
    for number, piece in enumerate(pieces):
        depth = piece.shape[0]
        first = pl.multiple_of(starts[number], 128)
        term = jnp.dot(rows_ref[:, pl.ds(first, depth)], piece[...], preferred_element_type=jnp.float32)
        total = term if total is None else total + term
    return total


def finish_kernel(count, has_total, starts, rows_ref, *refs):
    total_in = refs[0] if has_total else None
    refs = refs[int(has_total) :]
    pieces = refs[:count]
    cos_ref, sin_ref, marks_ref, clean_ref, noisy_ref = refs[count:]
    sums = gather_sum(starts, rows_ref, total_in, pieces)
    tokens = clean_ref.shape[0]
    width = clean_ref.shape[1]
    clean_sums = sums[:tokens]
    noisy_sums = jnp.where(marks_ref[...] == 1, sums[tokens : tokens + 1], clean_sums)
    cosine, sine = cos_ref[...], sin_ref[...]
    for part, out_ref in ((clean_sums, clean_ref), (noisy_sums, noisy_ref)):
        for lane in range(0, width // 2, HEAD_DIM):
            key = part[:, lane : lane + HEAD_DIM]
            rotated = key * cosine + pltpu.roll(key, HEAD_DIM // 2, 1) * sine
            out_ref[:, lane : lane + HEAD_DIM] = rotated.astype(jnp.bfloat16)
        out_ref[:, width // 2 :] = part[:, width // 2 :].astype(jnp.bfloat16)


def whole(array):
    zeros = (0,) * array.ndim
    return pl.BlockSpec(array.shape, lambda i, *_: zeros)


def project_partial(rows, total, pieces, starts):
    extra = [] if total is None else [total]
    width = pieces[0].shape[1]
    operands = [rows, *extra, *pieces]
    return pl.pallas_call(
        functools.partial(partial_kernel, len(pieces), total is not None),
        out_shape=jax.ShapeDtypeStruct((rows.shape[0], width), jnp.float32),
        grid_spec=pltpu.PrefetchScalarGridSpec(
            num_scalar_prefetch=1,
            grid=(1,),
            in_specs=[whole(a) for a in operands],
            out_specs=pl.BlockSpec((rows.shape[0], width), lambda i, *_: (0, 0)),
        ),
        compiler_params=pltpu.CompilerParams(vmem_limit_bytes=VMEM_LIMIT),
        name="project_partial",
    )(starts, *operands)


def project_finish(rows, total, pieces, starts, cosine, sine, marks):
    extra = [] if total is None else [total]
    width = pieces[0].shape[1]
    tokens = marks.shape[0]
    operands = [rows, *extra, *pieces, cosine, sine, marks]
    shape = jax.ShapeDtypeStruct((tokens, width), jnp.bfloat16)
    return pl.pallas_call(
        functools.partial(finish_kernel, len(pieces), total is not None),
        out_shape=(shape, shape),
        grid_spec=pltpu.PrefetchScalarGridSpec(
            num_scalar_prefetch=1,
            grid=(1,),
            in_specs=[whole(a) for a in operands],
            out_specs=[pl.BlockSpec((tokens, width), lambda i, *_: (0, 0))] * 2,
        ),
        compiler_params=pltpu.CompilerParams(vmem_limit_bytes=VMEM_LIMIT),
        name="project_finish",
    )(starts, *operands)


def scores_of(query, key):
    scores = lax.dot_general(query, key, (((1,), (1,)), ((), ())), preferred_element_type=jnp.float32)
    return scores * (HEAD_DIM**-0.5 * LOG2E)


def own_kernel(groups, flags, q_ref, ck_ref, cv_ref, nk_ref, nv_ref, acc_ref, stat_ref):
    core = flags[0]
    lanes = lax.broadcasted_iota(jnp.int32, (BLOCK, HEAD_DIM), 1)
    for head in range(groups):
        for side in range(2):
            mine = pl.ds(side * BLOCK, BLOCK)
            other = pl.ds((1 - side) * BLOCK, BLOCK)
            query = q_ref[mine, head * HEAD_DIM : (head + 1) * HEAD_DIM]
            near = scores_of(query, nk_ref[mine, :])
            far = scores_of(query, ck_ref[other, :])
            far = jnp.where(core == 1 - side, far, -1e30)
            top = jnp.maximum(jnp.max(near, -1, keepdims=True), jnp.max(far, -1, keepdims=True))
            near = jnp.exp2(near - top)
            far = jnp.where(core == 1 - side, jnp.exp2(far - top), 0.0)
            total = jnp.sum(near, -1, keepdims=True) + jnp.sum(far, -1, keepdims=True)
            mixed = jnp.dot(near.astype(jnp.bfloat16), nv_ref[mine, :], preferred_element_type=jnp.float32)
            mixed += jnp.dot(far.astype(jnp.bfloat16), cv_ref[other, :], preferred_element_type=jnp.float32)
            acc_ref[head, mine, :] = mixed
            stat_ref[head, mine, :] = jnp.where(lanes < HEAD_DIM // 2, top, total)


def later_kernel(groups, count, last, flags, q_ref, acc_in, stat_in, *refs):
    keys, values = refs[:count], refs[count : 2 * count]
    if last:
        own_out, other_out, acc_ref, stat_ref = refs[2 * count :]
    else:
        acc_ref, stat_ref = refs[2 * count :]
    acc_ref[...] = acc_in[...]
    stat_ref[...] = stat_in[...]
    lanes = lax.broadcasted_iota(jnp.int32, (BLOCK, HEAD_DIM), 1)

    for number in range(count):

        @pl.when(flags[number] == 1)
        def _(key_ref=keys[number], value_ref=values[number]):
            for head in range(groups):
                for side in range(2):
                    mine = pl.ds(side * BLOCK, BLOCK)
                    query = q_ref[mine, head * HEAD_DIM : (head + 1) * HEAD_DIM]
                    stat = stat_ref[head, mine, :]
                    top, total = stat[:, :1], stat[:, HEAD_DIM // 2 : HEAD_DIM // 2 + 1]
                    scores = scores_of(query, key_ref[...])
                    new_top = jnp.maximum(top, jnp.max(scores, -1, keepdims=True))
                    weights = jnp.exp2(scores - new_top)
                    rescale = jnp.exp2(top - new_top)
                    total = total * rescale + jnp.sum(weights, -1, keepdims=True)
                    mixed = jnp.dot(
                        weights.astype(jnp.bfloat16), value_ref[...], preferred_element_type=jnp.float32
                    )
                    acc_ref[head, mine, :] = acc_ref[head, mine, :] * rescale + mixed
                    stat_ref[head, mine, :] = jnp.where(lanes < HEAD_DIM // 2, new_top, total)

    if last:
        for head in range(groups):
            for side, out_ref in ((0, own_out), (1, other_out)):
                mine = pl.ds(side * BLOCK, BLOCK)
                total = stat_ref[head, mine, :][:, HEAD_DIM // 2 : HEAD_DIM // 2 + 1]
                out_ref[:, head * HEAD_DIM : (head + 1) * HEAD_DIM] = (
                    acc_ref[head, mine, :] / total
                ).astype(jnp.bfloat16)


def attention_shapes(query_rows, kv_heads):
    tokens, columns = query_rows.shape
    heads = columns // HEAD_DIM
    groups = heads // kv_heads
    q_spec = pl.BlockSpec((tokens, groups * HEAD_DIM), lambda g, *_: (0, g))
    state_spec = pl.BlockSpec((groups, tokens, HEAD_DIM), lambda g, *_: (g, 0, 0))
    state = jax.ShapeDtypeStruct((heads, tokens, HEAD_DIM), jnp.float32)
    return tokens, groups, q_spec, state_spec, state


def kv_specs(part, kv_heads):
    rows = part.shape[0]
    key_spec = pl.BlockSpec((rows, HEAD_DIM), lambda g, *_: (0, g))
    value_spec = pl.BlockSpec((rows, HEAD_DIM), lambda g, *_: (0, g + kv_heads))
    return key_spec, value_spec


def attend_own(flags, query_rows, clean, noisy, kv_heads):
    tokens, groups, q_spec, state_spec, state = attention_shapes(query_rows, kv_heads)
    key_spec, value_spec = kv_specs(clean, kv_heads)
    return pl.pallas_call(
        functools.partial(own_kernel, groups),
        out_shape=(state, state),
        grid_spec=pltpu.PrefetchScalarGridSpec(
            num_scalar_prefetch=1,
            grid=(kv_heads,),
            in_specs=[q_spec, key_spec, value_spec, key_spec, value_spec],
            out_specs=[state_spec, state_spec],
        ),
        compiler_params=pltpu.CompilerParams(vmem_limit_bytes=VMEM_LIMIT),
        name="attend_own",
    )(flags, query_rows, clean, clean, noisy, noisy)


def attend_later(flags, query_rows, running, parts, kv_heads, last):
    tokens, groups, q_spec, state_spec, state = attention_shapes(query_rows, kv_heads)
    specs = [kv_specs(part, kv_heads) for part in parts]
    if last:
        half = jax.ShapeDtypeStruct((tokens // 2, query_rows.shape[1]), jnp.bfloat16)
        half_spec = pl.BlockSpec((tokens // 2, groups * HEAD_DIM), lambda g, *_: (0, g))
        out_shape, out_specs = (half, half), [half_spec, half_spec]
        scratch = [pltpu.VMEM((groups, tokens, HEAD_DIM), jnp.float32)] * 2
    else:
        out_shape, out_specs, scratch = (state, state), [state_spec, state_spec], []
    return pl.pallas_call(
        functools.partial(later_kernel, groups, len(parts), last),
        out_shape=out_shape,
        grid_spec=pltpu.PrefetchScalarGridSpec(
            num_scalar_prefetch=1,
            grid=(kv_heads,),
            in_specs=[q_spec, state_spec, state_spec, *(s[0] for s in specs), *(s[1] for s in specs)],
            out_specs=out_specs,
            scratch_shapes=scratch,
        ),
        compiler_params=pltpu.CompilerParams(vmem_limit_bytes=VMEM_LIMIT),
        name="attend_last" if last else "attend_later",
    )(flags, query_rows, *running, *parts, *parts)


def shards(seq_size, fsdp_size, clean_states, noise_mask, mask_embed, queries, w_key, w_value):
    chips = seq_size // 2
    place = lax.axis_index("seq")
    core = lax.rem(place, 2)
    chip = place // 2
    shard = lax.axis_index("fsdp")
    states = clean_states[0]
    marks = noise_mask[0]
    query_own = queries[0]
    tokens = states.shape[0]
    depth, kv_width = w_key.shape
    half_width = kv_width // 2
    kv_heads = half_width // HEAD_DIM
    query_half = query_own.shape[1] // 2

    def swap_cores(array):
        return lax.ppermute(array, "seq", [(s, s ^ 1) for s in range(seq_size)])

    def to_chip(array, flip, sources=None):
        sources = range(chips) if sources is None else sources
        pairs = [(2 * s + c, 2 * (s ^ flip) + c) for s in sources for c in range(2)]
        return lax.ppermute(array, "seq", pairs)

    def to_shard(array, flip):
        return lax.ppermute(array, "fsdp", [(s, s ^ flip) for s in range(fsdp_size)])

    def weight_rows(first, count):
        return jnp.concatenate(
            [lax.dynamic_slice(w, (first, core * half_width), (count, half_width)) for w in (w_key, w_value)], 1
        )

    rounds = []
    if chips == 4:
        quarter = depth // chips
        mine = weight_rows(chip * quarter, quarter)
        arrived = [(shard ^ flip, to_shard(mine, flip)) for flip in range(1, fsdp_size)]
        for source, piece in arrived:
            along_x = to_chip(piece, 1)
            along_y = to_chip(piece, 2)
            corner_a = to_chip(along_x[: quarter // 2], 2)
            corner_b = to_chip(along_y[quarter // 2 :], 1)
            base = source * depth
            rounds.append(
                (
                    [piece, along_x, along_y, corner_a, corner_b],
                    [
                        base + chip * quarter,
                        base + (chip ^ 1) * quarter,
                        base + (chip ^ 2) * quarter,
                        base + (chip ^ 3) * quarter,
                        base + (chip ^ 3) * quarter + quarter // 2,
                    ],
                )
            )
        early = ([weight_rows(0, depth)], [shard * depth])
        for pieces, starts in rounds[:-1]:
            early = (early[0] + pieces, early[1] + starts)
        final = rounds[-1]
    else:
        early = None
        gathered = lax.all_gather(weight_rows(0, depth), "fsdp", axis=0, tiled=True)
        final = ([gathered], [jnp.int32(0)])

    def as_scalars(values):
        return jnp.stack([jnp.asarray(v, jnp.int32) for v in values])

    mask_rows = jnp.broadcast_to(mask_embed[None, :], (MASK_ROWS, mask_embed.shape[0]))
    rows = jnp.concatenate([states, swap_cores(states), mask_rows], 0)
    all_marks = jnp.concatenate([marks, swap_cores(marks)])[:, None]
    query_kept = lax.dynamic_slice(query_own, (0, core * query_half), (tokens, query_half))
    query_sent = lax.dynamic_slice(query_own, (0, (1 - core) * query_half), (tokens, query_half))
    query_rows = jnp.concatenate([query_kept, swap_cores(query_sent)], 0)
    steps = jnp.arange(tokens, dtype=jnp.int32)
    cosine, sine = rotation(jnp.concatenate([place * tokens + steps, (place ^ 1) * tokens + steps]))

    total = None if early is None else project_partial(rows, None, early[0], as_scalars(early[1]))
    clean, noisy = project_finish(rows, total, final[0], as_scalars(final[1]), cosine, sine, all_marks)

    if chips == 4:
        along_x = to_chip(clean, 1, (0, 1, 2))
        along_y = to_chip(clean, 2, (0, 1))
        half = clean.shape[0] // 2
        corner_a = to_chip(along_x[:half], 2, (0, 1))
        corner_b = to_chip(along_y[half:], 1, (2, 3))
        stages = [([along_x, along_y], [1, 2]), ([corner_a, corner_b], [3, 3])]
    else:
        stages = []
        for flip in range(1, chips):
            stages.append(([to_chip(clean, flip, [s for s in range(chips) if s < s ^ flip])], [flip]))
    running = attend_own(as_scalars([core]), query_rows, clean, noisy, kv_heads)
    for number, (parts, flips) in enumerate(stages):
        flags = as_scalars([(chip ^ flip) < chip for flip in flips])
        running = attend_later(flags, query_rows, running, parts, kv_heads, number == len(stages) - 1)
    own_out, other_out = running
    received = swap_cores(other_out)
    output = jnp.where(
        core == 0,
        jnp.concatenate([own_out, received], 1),
        jnp.concatenate([received, own_out], 1),
    )
    return output[None]


def solution(mesh):
    placed = (
        P("fsdp", "seq", None),
        P("fsdp", "seq"),
        P(),
        P("fsdp", "seq", None),
        P("fsdp", None),
        P("fsdp", None),
    )
    return jax.shard_map(
        functools.partial(shards, mesh.shape["seq"], mesh.shape["fsdp"]),
        mesh=mesh,
        in_specs=placed,
        out_specs=P("fsdp", "seq", None),
        check_vma=False,
    )
```

```python
import functools
import math

import jax
import jax.numpy as jnp
from jax import lax
from jax.experimental import pallas as pl
from jax.experimental.pallas import tpu as pltpu
from jax.sharding import PartitionSpec as P

HEADS = 16
HEAD_DIM = 128
BLOCK = 256
ROPE_BASE = 500000.0
MASK_ROWS = 16
SCORE_SCALE = HEAD_DIM**-0.5 * math.log2(math.e)
VMEM_LIMIT = 16 * 1024 * 1024

IN_VMEM = pl.BlockSpec(memory_space=pltpu.VMEM)
IN_SMEM = pl.BlockSpec(memory_space=pltpu.SMEM)
IN_PLACE = pl.BlockSpec(memory_space=pl.ANY)


def kernel_call(body, name, out_shape, in_specs, out_specs, scratch=(), aliases=None, flops=0):
    return pl.pallas_call(
        body,
        out_shape=out_shape,
        in_specs=in_specs,
        out_specs=out_specs,
        scratch_shapes=scratch,
        input_output_aliases=aliases or {},
        compiler_params=pltpu.CompilerParams(vmem_limit_bytes=VMEM_LIMIT),
        cost_estimate=pl.CostEstimate(flops=flops, bytes_accessed=0, transcendentals=0),
        name=name,
    )


def bf16(*shape):
    return jax.ShapeDtypeStruct(shape, jnp.bfloat16)


def f32(*shape):
    return jax.ShapeDtypeStruct(shape, jnp.float32)


def rotation(positions):
    half_dim = HEAD_DIM // 2
    frequency = ROPE_BASE ** (-(jnp.arange(half_dim, dtype=jnp.float32) * 2.0 / HEAD_DIM))
    angles = positions.astype(jnp.float32)[:, None] * frequency[None, :]
    cosine = jnp.cos(angles)
    sine = jnp.sin(angles)
    return jnp.concatenate([cosine, cosine], -1), jnp.concatenate([-sine, sine], -1)


def cut_kernel(where, key_ref, value_ref, *refs):
    outs, sem = refs[:-1], refs[-1]
    half = key_ref.shape[1] // 2
    first_column = pl.multiple_of(where[0] * half, HEAD_DIM)
    copies = []
    for number, out in enumerate(outs):
        count = out.shape[0]
        rows = pl.ds(pl.multiple_of(where[1 + number] * count, 16), count)
        for side, weight in enumerate((key_ref, value_ref)):
            copies.append(
                pltpu.make_async_copy(
                    weight.at[rows, pl.ds(first_column, half)],
                    out.at[:, side * half : (side + 1) * half],
                    sem.at[2 * number + side],
                )
            )
    for copy in copies:
        copy.start()
    for copy in copies:
        copy.wait()


def cut_weights(core, starts, counts, w_key, w_value):
    where = jnp.stack([jnp.asarray(v, jnp.int32) for v in (core, *starts)])
    return kernel_call(
        cut_kernel,
        "cut_weights",
        [bf16(count, w_key.shape[1]) for count in counts],
        [IN_SMEM, IN_PLACE, IN_PLACE],
        [IN_VMEM] * len(counts),
        [pltpu.SemaphoreType.DMA((2 * len(counts),))],
    )(where, w_key, w_value)


def stage_kernel(where, states_ref, embed_ref, query_ref, rows_ref, kept_ref, sent_ref, sem):
    core = where[0]
    tokens = states_ref.shape[0]
    half = query_ref.shape[1] // 2
    kept = pl.ds(pl.multiple_of(core * half, HEAD_DIM), half)
    sent = pl.ds(pl.multiple_of((1 - core) * half, HEAD_DIM), half)
    copies = [
        pltpu.make_async_copy(query_ref.at[:, sent], sent_ref, sem.at[0]),
        pltpu.make_async_copy(query_ref.at[:, kept], kept_ref, sem.at[1]),
        pltpu.make_async_copy(states_ref, rows_ref.at[pl.ds(0, tokens), :], sem.at[2]),
    ]
    for copy in copies:
        copy.start()
    rows_ref[pl.ds(tokens, MASK_ROWS), :] = jnp.broadcast_to(embed_ref[...], (MASK_ROWS, embed_ref.shape[1]))
    for copy in copies:
        copy.wait()


def stage(core, states, mask_embed, queries):
    tokens, width = states.shape
    half = queries.shape[1] // 2
    return kernel_call(
        stage_kernel,
        "stage",
        [bf16(tokens + MASK_ROWS, width), bf16(tokens, half), bf16(tokens, half)],
        [IN_SMEM, IN_PLACE, IN_VMEM, IN_PLACE],
        [IN_VMEM] * 3,
        [pltpu.SemaphoreType.DMA((3,))],
    )(jnp.asarray(core, jnp.int32)[None], states, mask_embed[None, :], queries)


def gather_sum(starts, rows_ref, total_in, pieces):
    total = None if total_in is None else total_in[...]
    for number, piece in enumerate(pieces):
        depth = piece.shape[0]
        first = pl.multiple_of(starts[number], HEAD_DIM)
        term = jnp.dot(rows_ref[:, pl.ds(first, depth)], piece[...], preferred_element_type=jnp.float32)
        total = term if total is None else total + term
    return total


def partial_kernel(count, starts, rows_a, rows_b, *refs):
    pieces, (total_a, total_b) = refs[:count], refs[count:]
    total_a[...] = gather_sum(starts, rows_a, None, pieces)
    total_b[...] = gather_sum(starts, rows_b, None, pieces)


def project_partial(rows, pieces, starts):
    width = pieces[0].shape[1]
    depth = sum(p.shape[0] for p in pieces)
    return kernel_call(
        functools.partial(partial_kernel, len(pieces)),
        "project_partial",
        [f32(r.shape[0], width) for r in rows],
        [IN_SMEM] + [IN_VMEM] * (2 + len(pieces)),
        [IN_VMEM] * 2,
        flops=2 * width * depth * sum(r.shape[0] for r in rows),
    )(starts, *rows, *pieces)


def finish_kernel(count, has_total, starts, rows_a, rows_b, *refs):
    total_a = total_b = None
    if has_total:
        total_a, total_b = refs[:2]
        refs = refs[2:]
    pieces = refs[:count]
    cos_ref, sin_ref, marks_a, marks_b, clean_ref, noisy_ref = refs[count:]
    tokens = rows_b.shape[0]
    width = clean_ref.shape[1]
    sums_a = gather_sum(starts, rows_a, total_a, pieces)
    sums_b = gather_sum(starts, rows_b, total_b, pieces)
    mask_sums = sums_a[tokens : tokens + 1]
    for side, sums, marks in ((0, sums_a[:tokens], marks_a), (1, sums_b, marks_b)):
        mine = pl.ds(side * tokens, tokens)
        cosine, sine = cos_ref[mine, :], sin_ref[mine, :]
        masked = marks[...] == 1
        for lane in range(0, width, HEAD_DIM):
            clean = sums[:, lane : lane + HEAD_DIM]
            noisy = jnp.where(masked, mask_sums[:, lane : lane + HEAD_DIM], clean)
            for part, out_ref in ((clean, clean_ref), (noisy, noisy_ref)):
                if lane < width // 2:
                    part = part * cosine + pltpu.roll(part, HEAD_DIM // 2, 1) * sine
                out_ref[mine, lane : lane + HEAD_DIM] = part.astype(jnp.bfloat16)


def project_finish(rows, totals, pieces, starts, cosine, sine, marks):
    width = pieces[0].shape[1]
    tokens = rows[1].shape[0]
    depth = sum(p.shape[0] for p in pieces)
    operands = [*rows, *totals, *pieces, cosine, sine, *marks]
    return kernel_call(
        functools.partial(finish_kernel, len(pieces), bool(totals)),
        "project_finish",
        [bf16(2 * tokens, width)] * 2,
        [IN_SMEM] + [IN_VMEM] * len(operands),
        [IN_VMEM] * 2,
        flops=2 * width * depth * sum(r.shape[0] for r in rows),
    )(starts, *operands)


def scores_of(query, key):
    return lax.dot_general(query, key, (((1,), (1,)), ((), ())), preferred_element_type=jnp.float32)


def lane_tiles(array):
    return [array[:, lane : lane + HEAD_DIM] for lane in range(0, array.shape[1], HEAD_DIM)]


def absorb(scores, values, before):
    tiles = [lane_tiles(s) for s in scores]
    peak = functools.reduce(jnp.maximum, [t for part in tiles for t in part])
    top = jnp.broadcast_to(jnp.max(peak, -1, keepdims=True), peak.shape) * SCORE_SCALE
    if before is not None:
        top = jnp.maximum(top, before[0])
    total = mixture = None
    for part, value in zip(tiles, values):
        weights = [jnp.exp2(t * SCORE_SCALE - top) for t in part]
        for weight in weights:
            total = weight if total is None else total + weight
        mixed = jnp.dot(
            jnp.concatenate([w.astype(jnp.bfloat16) for w in weights], 1), value, preferred_element_type=jnp.float32
        )
        mixture = mixed if mixture is None else mixture + mixed
    if before is not None:
        rescale = jnp.exp2(before[0] - top)
        total = before[1] * rescale + total
        mixture = before[2] * rescale + mixture
    return top, total, mixture


def pipelined(tasks, score, use):
    waiting = None
    for task in tasks:
        scores = score(task)
        if waiting is not None:
            use(*waiting)
        waiting = (task, scores)
    use(*waiting)


def own_kernel(kv_heads, where, q_a, q_b, clean_ref, noisy_ref, top_ref, sum_ref, mix_ref):
    core = where[0]
    tokens = q_a.shape[0]
    heads = q_a.shape[1] // HEAD_DIM
    groups = heads // kv_heads
    tasks = [(head, side) for head in range(heads) for side in range(2)]

    def lanes(head, value):
        first = (head // groups + (kv_heads if value else 0)) * HEAD_DIM
        return slice(first, first + HEAD_DIM)

    def score(task):
        head, side = task
        query = (q_a, q_b)[side][:, head * HEAD_DIM : (head + 1) * HEAD_DIM]
        near = scores_of(query, noisy_ref[side * tokens : (side + 1) * tokens, lanes(head, False)])
        far = scores_of(query, clean_ref[(1 - side) * tokens : (2 - side) * tokens, lanes(head, False)])
        return [near, jnp.where(core == 1 - side, far, -1e30)]

    def use(task, scores):
        head, side = task
        values = [
            noisy_ref[side * tokens : (side + 1) * tokens, lanes(head, True)],
            clean_ref[(1 - side) * tokens : (2 - side) * tokens, lanes(head, True)],
        ]
        top, total, mixture = absorb(scores, values, None)
        mine = pl.ds(side * tokens, tokens)
        top_ref[head, mine, :] = top
        sum_ref[head, mine, :] = total
        mix_ref[head, mine, :] = mixture

    pipelined(tasks, score, use)


def attend_own(core, queries, clean, noisy, kv_heads):
    tokens = queries[0].shape[0]
    heads = queries[0].shape[1] // HEAD_DIM
    return kernel_call(
        functools.partial(own_kernel, kv_heads),
        "attend_own",
        [f32(heads, 2 * tokens, HEAD_DIM)] * 3,
        [IN_SMEM] + [IN_VMEM] * 4,
        [IN_VMEM] * 3,
        flops=8 * heads * tokens * tokens * HEAD_DIM,
    )(jnp.asarray(core, jnp.int32)[None], *queries, clean, noisy)


def later_tasks(kv_heads, groups, heads, q_a, q_b, keys, state, store):
    tokens = q_a.shape[0]

    def lanes(head, value):
        first = (head // groups + (kv_heads if value else 0)) * HEAD_DIM
        return slice(first, first + HEAD_DIM)

    def score(task):
        head, side = task
        query = (q_a, q_b)[side][:, head * HEAD_DIM : (head + 1) * HEAD_DIM]
        return [scores_of(query, key[:, lanes(head, False)]) for key in keys]

    def use(task, scores):
        head, side = task
        mine = pl.ds(side * tokens, tokens)
        values = [key[:, lanes(head, True)] for key in keys]
        store(head, side, absorb(scores, values, state(head, mine)))

    pipelined([(head, side) for head in heads for side in range(2)], score, use)


def later_kernel(kv_heads, count, flags, q_a, q_b, *refs):
    parts, refs = refs[:count], refs[count:]
    outs = refs[3:]
    heads = q_a.shape[1] // HEAD_DIM
    tokens = q_a.shape[0]

    def state(head, mine):
        return tuple(out[head, mine, :] for out in outs)

    def store(head, side, values):
        for out, value in zip(outs, values):
            out[head, pl.ds(side * tokens, tokens), :] = value

    for number in range(count):

        @pl.when(flags[number] == 1)
        def _(part=parts[number]):
            later_tasks(kv_heads, heads // kv_heads, range(heads), q_a, q_b, [part], state, store)


def attend_later(flags, queries, parts, running, kv_heads):
    tokens = queries[0].shape[0]
    heads = queries[0].shape[1] // HEAD_DIM
    count = len(parts)
    return kernel_call(
        functools.partial(later_kernel, kv_heads, count),
        "attend_later",
        [f32(heads, 2 * tokens, HEAD_DIM)] * 3,
        [IN_SMEM] + [IN_VMEM] * (5 + count),
        [IN_VMEM] * 3,
        aliases={3 + count + i: i for i in range(3)},
        flops=8 * heads * tokens * sum(p.shape[0] for p in parts) * HEAD_DIM,
    )(flags, *queries, *parts, *running)


def last_kernel(kv_heads, heads, count, flags, q_a, q_b, *refs):
    parts, state_refs, outs = refs[:count], refs[count : count + 3], refs[count + 3 :]
    groups = q_a.shape[1] // HEAD_DIM // kv_heads

    def state(head, mine):
        return tuple(ref[head, mine, :] for ref in state_refs)

    def store(head, side, values):
        _, total, mixture = values
        total = jnp.sum(total, -1, keepdims=True)
        place = (head - heads[0]) * HEAD_DIM
        outs[side][:, place : place + HEAD_DIM] = (mixture / total).astype(jnp.bfloat16)

    @pl.when(flags[0] == 1)
    def _():
        later_tasks(kv_heads, groups, heads, q_a, q_b, parts, state, store)

    @pl.when(flags[0] != 1)
    def _():
        for head in heads:
            for side in range(2):
                store(head, side, state(head, pl.ds(side * q_a.shape[0], q_a.shape[0])))


def attend_last(flags, queries, parts, running, kv_heads, heads):
    tokens = queries[0].shape[0]
    count = len(parts)
    return kernel_call(
        functools.partial(last_kernel, kv_heads, heads, count),
        "attend_last",
        [bf16(tokens, len(heads) * HEAD_DIM)] * 2,
        [IN_SMEM] + [IN_VMEM] * (5 + count),
        [IN_VMEM] * 2,
        flops=8 * len(heads) * tokens * sum(p.shape[0] for p in parts) * HEAD_DIM,
    )(flags, *queries, *parts, *running)


def place_kernel(count, where, *refs):
    parts, out, sem = refs[: 2 * count], refs[2 * count], refs[2 * count + 1]
    core = where[0]
    half = out.shape[1] // 2
    width = half // count
    copies = []
    for number, part in enumerate(parts):
        side = core if number < count else 1 - core
        first = pl.multiple_of(side * half + (number % count) * width, HEAD_DIM)
        copies.append(pltpu.make_async_copy(part, out.at[:, pl.ds(first, width)], sem.at[number]))
    for copy in copies:
        copy.start()
    for copy in copies:
        copy.wait()


def place_heads(core, mine, received):
    count = len(mine)
    tokens, width = mine[0].shape
    return kernel_call(
        functools.partial(place_kernel, count),
        "place_heads",
        bf16(tokens, 2 * count * width),
        [IN_SMEM] + [IN_VMEM] * (2 * count),
        IN_PLACE,
        [pltpu.SemaphoreType.DMA((2 * count,))],
    )(jnp.asarray(core, jnp.int32)[None], *mine, *received)


def as_scalars(values):
    return jnp.stack([jnp.asarray(v, jnp.int32) for v in values])


def shards(seq_size, fsdp_size, clean_states, noise_mask, mask_embed, queries, w_key, w_value):
    chips = seq_size // 2
    place = lax.axis_index("seq")
    core = lax.rem(place, 2)
    chip = place // 2
    shard = lax.axis_index("fsdp")
    states = clean_states[0]
    marks = noise_mask[0]
    tokens = states.shape[0]
    depth, kv_width = w_key.shape
    kv_heads = kv_width // 2 // HEAD_DIM
    square = chips == 4 and fsdp_size == 4

    def swap_cores(array):
        return lax.ppermute(array, "seq", [(s, s ^ 1) for s in range(seq_size)])

    def to_chip(array, flip, sources=None):
        sources = range(chips) if sources is None else sources
        pairs = [(2 * s + c, 2 * (s ^ flip) + c) for s in sources for c in range(2)]
        return lax.ppermute(array, "seq", pairs)

    def to_shard(array, flip):
        return lax.ppermute(array, "fsdp", [(s, s ^ flip) for s in range(fsdp_size)])

    if square:
        quarter = depth // chips
        mine, corner = cut_weights(core, (chip, chip ^ 3), (quarter, quarter), w_key, w_value)
        far, near, middle = to_shard(mine, 3), to_shard(mine, 1), to_shard(mine, 2)
        near_corner = to_shard(corner, 1)

    rows_a, query_a, query_sent = stage(core, states, mask_embed, queries[0])
    rows = (rows_a, swap_cores(states))
    query_rows = (query_a, swap_cores(query_sent))
    all_marks = [jnp.broadcast_to(m[:, None], (tokens, HEAD_DIM)) for m in (marks, swap_cores(marks))]
    steps = jnp.arange(tokens, dtype=jnp.int32)
    cosine, sine = rotation(jnp.concatenate([place * tokens + steps, (place ^ 1) * tokens + steps]))
    (own_half,) = cut_weights(core, (0,), (depth,), w_key, w_value)

    if square:
        far, own_half, cosine, sine, rows_a = lax.optimization_barrier((far, own_half, cosine, sine, rows_a))
        rows = (rows_a, rows[1])

        def plane(piece, source, diagonal):
            others = [to_chip(piece, 1), to_chip(piece, 2), to_chip(piece, 3) if diagonal is None else diagonal]
            return [piece, *others], [source * depth + (chip ^ flip) * quarter for flip in range(4)]

        first = plane(far, shard ^ 3, None)
        second = plane(near, shard ^ 1, near_corner)
        final = plane(middle, shard ^ 2, None)
        totals = project_partial(
            rows, [own_half] + first[0] + second[0], as_scalars([shard * depth] + first[1] + second[1])
        )
    else:
        totals = ()
        final = ([lax.all_gather(own_half, "fsdp", axis=0, tiled=True)], [jnp.int32(0)])
    clean, noisy = project_finish(rows, totals, final[0], as_scalars(final[1]), cosine, sine, all_marks)

    if square:
        along_x = to_chip(clean, 1, (0, 1, 2))
        along_y = to_chip(clean, 2, (0, 1))
        running = attend_own(core, query_rows, clean, noisy, kv_heads)
        along_x, along_y, running = lax.optimization_barrier((along_x, along_y, running))
        last_parts = [to_chip(along_x[:tokens], 2, (0, 1)), to_chip(along_y[tokens:], 1, (2, 3))]
        flags = as_scalars([(chip ^ flip) < chip for flip in (1, 2)])
        running = attend_later(flags, query_rows, [along_x, along_y], running, kv_heads)
        last_flip = 3
    else:
        running = attend_own(core, query_rows, clean, noisy, kv_heads)
        for flip in range(1, chips):
            part = to_chip(clean, flip, [s for s in range(chips) if s < s ^ flip])
            if flip < chips - 1:
                running = attend_later(as_scalars([(chip ^ flip) < chip]), query_rows, [part], running, kv_heads)
        last_parts, last_flip = [part], chips - 1
    flags = as_scalars([(chip ^ last_flip) < chip])
    kept, received = [], []
    heads = query_a.shape[1] // HEAD_DIM
    for first_head in range(0, heads, heads // kv_heads):
        own, other = attend_last(
            flags, query_rows, last_parts, running, kv_heads, range(first_head, first_head + heads // kv_heads)
        )
        kept.append(own)
        received.append(swap_cores(other))
    return place_heads(core, kept, received)[None]


def solution(mesh):
    placed = (
        P("fsdp", "seq", None),
        P("fsdp", "seq"),
        P(),
        P("fsdp", "seq", None),
        P("fsdp", None),
        P("fsdp", None),
    )
    return jax.shard_map(
        functools.partial(shards, mesh.shape["seq"], mesh.shape["fsdp"]),
        mesh=mesh,
        in_specs=placed,
        out_specs=P("fsdp", "seq", None),
        check_vma=False,
    )
```

```python
import functools
import math

import jax
import jax.numpy as jnp
from jax import lax
from jax.experimental import pallas as pl
from jax.experimental.pallas import tpu as pltpu
from jax.sharding import PartitionSpec as P

HEADS = 16
HEAD_DIM = 128
BLOCK = 256
ROPE_BASE = 500000.0
MASK_ROWS = 16
CHIPS = 4
SCORE_SCALE = HEAD_DIM**-0.5 * math.log2(math.e)
VMEM_LIMIT = 12 * 1024 * 1024
WIDE_LIMIT = 56 * 1024 * 1024

IN_VMEM = pl.BlockSpec(memory_space=pltpu.VMEM)
IN_SMEM = pl.BlockSpec(memory_space=pltpu.SMEM)
IN_PLACE = pl.BlockSpec(memory_space=pl.ANY)


def kernel_call(body, name, out_shape, in_specs, out_specs, scratch=(), aliases=None, flops=0, limit=VMEM_LIMIT):
    return pl.pallas_call(
        body,
        out_shape=out_shape,
        in_specs=in_specs,
        out_specs=out_specs,
        scratch_shapes=scratch,
        input_output_aliases=aliases or {},
        compiler_params=pltpu.CompilerParams(vmem_limit_bytes=limit),
        cost_estimate=pl.CostEstimate(flops=flops, bytes_accessed=0, transcendentals=0),
        name=name,
    )


def bf16(*shape):
    return jax.ShapeDtypeStruct(shape, jnp.bfloat16)


def f32(*shape):
    return jax.ShapeDtypeStruct(shape, jnp.float32)


def rotation(positions):
    half_dim = HEAD_DIM // 2
    frequency = ROPE_BASE ** (-(jnp.arange(half_dim, dtype=jnp.float32) * 2.0 / HEAD_DIM))
    angles = positions.astype(jnp.float32)[:, None] * frequency[None, :]
    cosine = jnp.cos(angles)
    sine = jnp.sin(angles)
    return jnp.concatenate([cosine, cosine], -1), jnp.concatenate([-sine, sine], -1)


def run_copies(copies):
    for copy in copies:
        copy.start()
    for copy in copies:
        copy.wait()


def core_columns(where, weight):
    half = weight.shape[1] // 2
    return pl.ds(pl.multiple_of(where[0] * half, HEAD_DIM), half)


def cut_kernel(flips, where, key_ref, value_ref, *refs):
    outs, sem = refs[:-1], refs[-1]
    columns = core_columns(where, key_ref)
    copies = []
    for out, flip in zip(outs, flips):
        size, width = out.shape
        first = 0 if flip is None else pl.multiple_of((where[1] ^ flip) * size, 16)
        for side, weight in enumerate((key_ref, value_ref)):
            target = out.at[:, side * (width // 2) : (side + 1) * (width // 2)]
            copies.append(pltpu.make_async_copy(weight.at[pl.ds(first, size), columns], target, sem.at[len(copies)]))
    run_copies(copies)


def cut_weights(where, flips, size, w_key, w_value):
    return kernel_call(
        functools.partial(cut_kernel, flips),
        "cut_weights",
        [bf16(size, w_key.shape[1])] * len(flips),
        [IN_SMEM, IN_PLACE, IN_PLACE],
        [IN_VMEM] * len(flips),
        [pltpu.SemaphoreType.DMA((2 * len(flips),))],
        limit=WIDE_LIMIT,
    )(where, w_key, w_value)


def fetch(segments, where, rows, refs, rows_held, held, sem):
    refs = list(refs)
    place = number = 0
    waits = []
    for pieces in segments:
        copies = []
        start_at = place
        for shard_flip, chip_flip, depth, size, as_given in pieces:
            first = 0 if shard_flip is None else (where[2] ^ shard_flip) * depth
            if chip_flip is not None:
                first = first + (where[1] ^ chip_flip) * size
            columns = pl.ds(first if isinstance(first, int) else pl.multiple_of(first, HEAD_DIM), size)
            into = slice(place, place + size)
            low = 0
            for part in rows:
                copies.append((part.at[:, columns], rows_held.at[low : low + part.shape[0], into]))
                low += part.shape[0]
            if as_given:
                for side in range(2):
                    weight = refs.pop(0)
                    half = weight.shape[1] // 2
                    target = held.at[into, side * half : (side + 1) * half]
                    copies.append((weight.at[:, core_columns(where, weight)], target))
            else:
                copies.append((refs.pop(0), held.at[into, :]))
            place += size
        copies = [pltpu.make_async_copy(a, b, sem.at[number + i]) for i, (a, b) in enumerate(copies)]
        number += len(copies)
        for copy in copies:
            copy.start()
        waits.append((copies, slice(start_at, place)))
    return waits


def products(waits, rows_held, held, total):
    for copies, into in waits:
        for copy in copies:
            copy.wait()
        term = jnp.dot(rows_held[:, into], held[into, :], preferred_element_type=jnp.float32)
        total = term if total is None else total + term
    return total


def partial_kernel(segments, count, where, states, other, masks, *refs):
    total_ref, rows_held, held, sem = refs[count:]
    waits = fetch(segments, where, (states, other, masks), refs[:count], rows_held, held, sem)
    total_ref[...] = products(waits, rows_held, held, None)


def finish_kernel(segments, count, has_total, where, states, other, masks, *refs):
    pieces, refs = refs[:count], refs[count:]
    total_ref = refs[0] if has_total else None
    cos_ref, sin_ref, marks_a, marks_b, *outs = refs[int(has_total) :]
    *outs, rows_held, held, kept, sem, out_sem = outs
    waits = fetch(segments, where, (states, other, masks), pieces, rows_held, held, sem)
    tokens = other.shape[0]
    masked = [jnp.broadcast_to(m[...].astype(jnp.float32), (HEAD_DIM, tokens)).T > 0.5 for m in (marks_a, marks_b)]
    sums = products(waits, rows_held, held, None if total_ref is None else total_ref[...])
    kv_heads = len(outs) // 2
    mask_sums = sums[2 * tokens : 2 * tokens + 1]
    writes = []
    for head in range(kv_heads):
        for side in range(2):
            mine = slice(side * tokens, (side + 1) * tokens)
            for is_value in range(2):
                first = (is_value * kv_heads + head) * HEAD_DIM
                clean = sums[mine, first : first + HEAD_DIM]
                noisy = jnp.where(masked[side], mask_sums[:, first : first + HEAD_DIM], clean)
                for copy, part in enumerate((clean, noisy)):
                    if not is_value:
                        part = part * cos_ref[mine, :] + pltpu.roll(part, HEAD_DIM // 2, 1) * sin_ref[mine, :]
                    into = slice(is_value * HEAD_DIM, (is_value + 1) * HEAD_DIM)
                    kept[copy, head, mine, into] = part.astype(jnp.bfloat16)
        for copy in range(2):
            number = copy * kv_heads + head
            writes.append(pltpu.make_async_copy(kept.at[copy, head], outs[number], out_sem.at[number]))
            writes[-1].start()
    for write in writes:
        write.wait()


def project(rows, segments, where, total=None, ending=None):
    kinds, pieces = [], []
    copies = 0
    for segment in segments:
        kinds.append([])
        for piece, shard_flip, chip_flip, depth in segment:
            as_given = isinstance(piece, tuple)
            pieces.extend(piece if as_given else (piece,))
            kinds[-1].append((shard_flip, chip_flip, depth, pieces[-1].shape[0], as_given))
            copies += 5 if as_given else 4
    width = pieces[0].shape[1]
    height = sum(r.shape[0] for r in rows)
    tokens = rows[0].shape[0]
    inner = sum(kind[3] for segment in kinds for kind in segment)
    held = [
        pltpu.VMEM((height, inner), jnp.bfloat16),
        pltpu.VMEM((inner, width), jnp.bfloat16),
    ]
    sems = pltpu.SemaphoreType.DMA((copies,))
    flops = 2 * width * inner * height
    specs = [IN_SMEM] + [IN_PLACE] * (3 + len(pieces))
    if ending is None:
        return kernel_call(
            functools.partial(partial_kernel, kinds, len(pieces)),
            "project_partial",
            f32(height, width),
            specs,
            IN_VMEM,
            [*held, sems],
            flops=flops,
        )(where, *rows, *pieces)
    kv_heads = width // 2 // HEAD_DIM
    extra = [*(() if total is None else (total,)), *ending]
    outs = kernel_call(
        functools.partial(finish_kernel, kinds, len(pieces), total is not None),
        "project_finish",
        [bf16(2 * tokens, 2 * HEAD_DIM)] * (2 * kv_heads),
        specs + [IN_VMEM] * len(extra),
        [IN_PLACE] * (2 * kv_heads),
        [
            *held,
            pltpu.VMEM((2, kv_heads, 2 * tokens, 2 * HEAD_DIM), jnp.bfloat16),
            sems,
            pltpu.SemaphoreType.DMA((2 * kv_heads,)),
        ],
        flops=flops,
    )(where, *rows, *pieces, *extra)
    return outs[:kv_heads], outs[kv_heads:]


def scores_of(query, key):
    return lax.dot_general(query, key, (((1,), (1,)), ((), ())), preferred_element_type=jnp.float32)


def lane_tiles(array):
    return [array[:, lane : lane + HEAD_DIM] for lane in range(0, array.shape[1], HEAD_DIM)]


def absorb(scores, values, before):
    tiles = [lane_tiles(s) for s in scores]
    peak = functools.reduce(jnp.maximum, [t for part in tiles for t in part])
    top = jnp.broadcast_to(jnp.max(peak, -1, keepdims=True), peak.shape) * SCORE_SCALE
    if before is not None:
        top = jnp.maximum(top, before[0])
    total = mixture = None
    for part, value in zip(tiles, values):
        weights = [jnp.exp2(t * SCORE_SCALE - top) for t in part]
        for weight in weights:
            total = weight if total is None else total + weight
        mixed = jnp.dot(
            jnp.concatenate([w.astype(jnp.bfloat16) for w in weights], 1), value, preferred_element_type=jnp.float32
        )
        mixture = mixed if mixture is None else mixture + mixed
    if before is not None:
        rescale = jnp.exp2(before[0] - top)
        total = before[1] * rescale + total
        mixture = before[2] * rescale + mixture
    return top, total, mixture


def pipelined(tasks, score, use):
    waiting = None
    for task in tasks:
        scores = score(task)
        if waiting is not None:
            use(*waiting)
        waiting = (task, scores)
    use(*waiting)


def query_of(query_ref, core, head):
    first = core * (query_ref.shape[1] // 2) + head * HEAD_DIM
    return query_ref[:, pl.ds(pl.multiple_of(first, HEAD_DIM), HEAD_DIM)]


def own_kernel(head_first, groups, where, q_a, q_b, clean_in, noisy_in, *refs):
    *state, clean_ref, noisy_ref, sem = refs
    core = where[0]
    tokens = q_a.shape[0]
    run_copies(
        [
            pltpu.make_async_copy(noisy_in, noisy_ref, sem.at[0]),
            pltpu.make_async_copy(clean_in, clean_ref, sem.at[1]),
        ]
    )

    def score(task):
        head, side = task
        query = query_of((q_a, q_b)[side], core, head_first + head)
        near = scores_of(query, noisy_ref[side * tokens : (side + 1) * tokens, :HEAD_DIM])
        far = scores_of(query, clean_ref[(1 - side) * tokens : (2 - side) * tokens, :HEAD_DIM])
        return [near, jnp.where(core == 1 - side, far, -1e30)]

    def use(task, scores):
        head, side = task
        values = [
            noisy_ref[side * tokens : (side + 1) * tokens, HEAD_DIM:],
            clean_ref[(1 - side) * tokens : (2 - side) * tokens, HEAD_DIM:],
        ]
        mine = pl.ds(side * tokens, tokens)
        for ref, value in zip(state, absorb(scores, values, None)):
            ref[head, mine, :] = value

    pipelined([(head, side) for head in range(groups) for side in range(2)], score, use)


def attend_own(where, queries, clean, noisy, head_first, groups):
    tokens = queries[0].shape[0]
    return kernel_call(
        functools.partial(own_kernel, head_first, groups),
        "attend_own",
        [f32(groups, 2 * tokens, HEAD_DIM)] * 3,
        [IN_SMEM] + [IN_VMEM] * 2 + [IN_PLACE] * 2,
        [IN_VMEM] * 3,
        [pltpu.VMEM(clean.shape, jnp.bfloat16)] * 2 + [pltpu.SemaphoreType.DMA((2,))],
        flops=16 * groups * tokens * tokens * HEAD_DIM,
    )(where, *queries, clean, noisy)


def later_tasks(core, head_first, groups, q_a, q_b, parts, state, store):
    tokens = q_a.shape[0]

    def score(task):
        head, side = task
        query = query_of((q_a, q_b)[side], core, head_first + head)
        return [scores_of(query, part[:, :HEAD_DIM]) for part in parts]

    def use(task, scores):
        head, side = task
        before = state(head, pl.ds(side * tokens, tokens))
        store(head, side, absorb(scores, [part[:, HEAD_DIM:] for part in parts], before))

    pipelined([(head, side) for head in range(groups) for side in range(2)], score, use)


def is_earlier(where, flip):
    return (where[1] ^ flip) < where[1]


def later_kernel(head_first, groups, flips, where, q_a, q_b, *refs):
    count = len(flips)
    parts, outs = refs[:count], refs[count + 3 :]
    tokens = q_a.shape[0]

    def state(head, mine):
        return tuple(out[head, mine, :] for out in outs)

    def store(head, side, values):
        for out, value in zip(outs, values):
            out[head, pl.ds(side * tokens, tokens), :] = value

    for chosen in range(1, 1 << count):
        wanted = [bool(chosen >> number & 1) for number in range(count)]
        hits = [is_earlier(where, flip) if want else ~is_earlier(where, flip) for flip, want in zip(flips, wanted)]

        @pl.when(functools.reduce(jnp.logical_and, hits))
        def _(used=[part for part, want in zip(parts, wanted) if want]):
            later_tasks(where[0], head_first, groups, q_a, q_b, used, state, store)


def attend_later(where, queries, parts, flips, running, head_first, groups):
    tokens = queries[0].shape[0]
    count = len(parts)
    return kernel_call(
        functools.partial(later_kernel, head_first, groups, flips),
        "attend_later",
        [f32(groups, 2 * tokens, HEAD_DIM)] * 3,
        [IN_SMEM] + [IN_VMEM] * (5 + count),
        [IN_VMEM] * 3,
        aliases={3 + count + i: i for i in range(3)},
        flops=8 * groups * tokens * sum(p.shape[0] for p in parts) * HEAD_DIM,
    )(where, *queries, *parts, *running)


def last_kernel(head_first, groups, count, flip, where, q_a, q_b, *refs):
    parts, state_refs, outs = refs[:count], refs[count : count + 3], refs[count + 3 :]
    tokens = q_a.shape[0]

    def state(head, mine):
        return tuple(ref[head, mine, :] for ref in state_refs)

    def store(head, side, values):
        _, total, mixture = values
        total = jnp.sum(total, -1, keepdims=True)
        outs[side][:, head * HEAD_DIM : (head + 1) * HEAD_DIM] = (mixture / total).astype(jnp.bfloat16)

    @pl.when(is_earlier(where, flip))
    def _():
        later_tasks(where[0], head_first, groups, q_a, q_b, parts, state, store)

    @pl.when(~is_earlier(where, flip))
    def _():
        for head in range(groups):
            for side in range(2):
                store(head, side, state(head, pl.ds(side * tokens, tokens)))


def attend_last(where, queries, parts, flip, running, head_first, groups):
    tokens = queries[0].shape[0]
    count = len(parts)
    return kernel_call(
        functools.partial(last_kernel, head_first, groups, count, flip),
        "attend_last",
        [bf16(tokens, groups * HEAD_DIM)] * 2,
        [IN_SMEM] + [IN_VMEM] * (5 + count),
        [IN_VMEM] * 2,
        flops=8 * groups * tokens * sum(p.shape[0] for p in parts) * HEAD_DIM,
    )(where, *queries, *parts, *running)


def place_kernel(count, where, *refs):
    parts, out, sem = refs[: 2 * count], refs[2 * count], refs[2 * count + 1]
    core = where[0]
    half = out.shape[1] // 2
    width = half // count
    copies = []
    for number, part in enumerate(parts):
        side = core if number < count else 1 - core
        first = pl.multiple_of(side * half + (number % count) * width, HEAD_DIM)
        copies.append(pltpu.make_async_copy(part, out.at[:, pl.ds(first, width)], sem.at[number]))
    for copy in copies:
        copy.start()
    for copy in copies:
        copy.wait()


def place_heads(where, mine, received):
    count = len(mine)
    tokens, width = mine[0].shape
    return kernel_call(
        functools.partial(place_kernel, count),
        "place_heads",
        bf16(tokens, 2 * count * width),
        [IN_SMEM] + [IN_VMEM] * (2 * count),
        IN_PLACE,
        [pltpu.SemaphoreType.DMA((2 * count,))],
    )(where, *mine, *received)


def as_scalars(values):
    return jnp.stack([jnp.asarray(v, jnp.int32) for v in values])


def shards(seq_size, fsdp_size, clean_states, noise_mask, mask_embed, queries, w_key, w_value):
    chips = seq_size // 2
    place = lax.axis_index("seq")
    core = lax.rem(place, 2)
    chip = place // 2
    shard = lax.axis_index("fsdp")
    states = clean_states[0]
    marks = noise_mask
    tokens = states.shape[0]
    depth, kv_width = w_key.shape
    kv_heads = kv_width // 2 // HEAD_DIM

    def swap_cores(array):
        return lax.ppermute(array, "seq", [(s, s ^ 1) for s in range(seq_size)])

    def to_chip(array, flip, sources=None):
        sources = range(chips) if sources is None else sources
        pairs = [(2 * s + c, 2 * (s ^ flip) + c) for s in sources for c in range(2)]
        return lax.ppermute(array, "seq", pairs)

    def to_shard(array, flip):
        return lax.ppermute(array, "fsdp", [(s, s ^ flip) for s in range(fsdp_size)])

    square = chips == CHIPS and fsdp_size == 4
    barrier = lax.optimization_barrier
    where = as_scalars([core, chip, shard])
    query_own = queries[0]
    if square:
        quarter = depth // chips
        (mine,) = cut_weights(where, (0,), quarter, w_key, w_value)
        far, near = to_shard(mine, 3), to_shard(mine, 1)

    mask_rows = jnp.broadcast_to(mask_embed[None, :], (MASK_ROWS, mask_embed.shape[0]))
    rows = (states, swap_cores(states), mask_rows)
    query_rows = (query_own, swap_cores(query_own))
    both_marks = (marks, swap_cores(marks))
    steps = jnp.arange(tokens, dtype=jnp.int32)
    cosine, sine = rotation(jnp.concatenate([place * tokens + steps, (place ^ 1) * tokens + steps]))

    if square:
        (corner,) = cut_weights(where, (3,), quarter, w_key, w_value)
        far, near, mine, corner, rows, query_rows, both_marks, cosine, sine = barrier(
            (far, near, mine, corner, rows, query_rows, both_marks, cosine, sine)
        )
        middle = to_shard(mine, 2)
        near_x, far_x = to_chip(near, 1), to_chip(far, 1)
        near_y, far_y = to_chip(near, 2), to_chip(far, 2)
        middle, corner, near_x, near_y, far_x, far_y = barrier((middle, corner, near_x, near_y, far_x, far_y))
        last = [to_chip(middle, flip) for flip in (3, 1, 2)]
        far_corner, near_corner = to_shard(corner, 3), to_shard(corner, 1)
        segments = [
            [((w_key, w_value), 0, None, depth)],
            [
                (far, 3, 0, depth),
                (far_x, 3, 1, depth),
                (far_y, 3, 2, depth),
            ],
            [(near, 1, 0, depth), (near_x, 1, 1, depth), (near_y, 1, 2, depth)],
        ]
        final = [
            [
                (middle, 2, 0, depth),
                (last[0], 2, 3, depth),
                (last[1], 2, 1, depth),
                (last[2], 2, 2, depth),
                (near_corner, 1, 3, depth),
                (far_corner, 3, 3, depth),
            ]
        ]
        total = project(rows, segments, where)
    else:
        (half_weights,) = cut_weights(where, (None,), depth, w_key, w_value)
        gathered = lax.all_gather(half_weights, "fsdp", axis=0, tiled=True)
        final, total = [[(gathered, None, None, depth)]], None
    clean, noisy = project(rows, final, where, total, (cosine, sine, *both_marks))

    groups = query_own.shape[1] // 2 // HEAD_DIM // kv_heads

    def corner_chip(along_x, along_y):
        return [to_chip(along_x[:tokens], 2, (0, 1)), to_chip(along_y[tokens:], 1, (2, 3))]

    heads = range(kv_heads)
    clean, noisy = list(clean), list(noisy)
    running, last_parts = [None] * kv_heads, [None] * kv_heads
    if square:
        along_x = [to_chip(part, 1, (0, 1, 2)) for part in clean]
        along_y = [to_chip(part, 2, (0, 1)) for part in clean]
        along = list(zip(along_x, along_y))
        for head in heads:
            running[head] = attend_own(where, query_rows, clean[head], noisy[head], head * groups, groups)
            along[head], running[head], noisy = barrier((along[head], running[head], noisy))
            last_parts[head] = corner_chip(*along[head])
        for head in heads:
            running[head] = attend_later(where, query_rows, along[head], (1, 2), running[head], head * groups, groups)
    else:
        for head in heads:
            running[head] = attend_own(where, query_rows, clean[head], noisy[head], head * groups, groups)
            for flip in range(1, chips):
                part = to_chip(clean[head], flip, [s for s in range(chips) if s < s ^ flip])
                if flip < chips - 1:
                    running[head] = attend_later(
                        where, query_rows, [part], (flip,), running[head], head * groups, groups
                    )
            last_parts[head] = [part]
    kept, received = [], []
    for head in heads:
        own, other = attend_last(
            where, query_rows, last_parts[head], chips - 1, running[head], head * groups, groups
        )
        kept.append(own)
        received.append(swap_cores(other))
    return place_heads(where, kept, received)[None]


def solution(mesh):
    placed = (
        P("fsdp", "seq", None),
        P("fsdp", "seq"),
        P(),
        P("fsdp", "seq", None),
        P("fsdp", None),
        P("fsdp", None),
    )
    return jax.shard_map(
        functools.partial(shards, mesh.shape["seq"], mesh.shape["fsdp"]),
        mesh=mesh,
        in_specs=placed,
        out_specs=P("fsdp", "seq", None),
        check_vma=False,
    )
```

```python
import functools
import math

import jax
import jax.numpy as jnp
from jax import lax
from jax.experimental import pallas as pl
from jax.experimental.pallas import tpu as pltpu
from jax.sharding import PartitionSpec as P

HEADS = 16
HEAD_DIM = 128
BLOCK = 256
ROPE_BASE = 500000.0
MASK_ROWS = 16
CHIPS = 4
SCORE_SCALE = HEAD_DIM**-0.5 * math.log2(math.e)
VMEM_LIMIT = 12 * 1024 * 1024
WIDE_LIMIT = 56 * 1024 * 1024

IN_VMEM = pl.BlockSpec(memory_space=pltpu.VMEM)
IN_SMEM = pl.BlockSpec(memory_space=pltpu.SMEM)
IN_PLACE = pl.BlockSpec(memory_space=pl.ANY)


def kernel_call(body, name, out_shape, in_specs, out_specs, scratch=(), aliases=None, flops=0, limit=VMEM_LIMIT):
    return pl.pallas_call(
        body,
        out_shape=out_shape,
        in_specs=in_specs,
        out_specs=out_specs,
        scratch_shapes=scratch,
        input_output_aliases=aliases or {},
        compiler_params=pltpu.CompilerParams(vmem_limit_bytes=limit),
        cost_estimate=pl.CostEstimate(flops=flops, bytes_accessed=0, transcendentals=0),
        name=name,
    )


def bf16(*shape):
    return jax.ShapeDtypeStruct(shape, jnp.bfloat16)


def f32(*shape):
    return jax.ShapeDtypeStruct(shape, jnp.float32)


def rotation(positions):
    half_dim = HEAD_DIM // 2
    frequency = ROPE_BASE ** (-(jnp.arange(half_dim, dtype=jnp.float32) * 2.0 / HEAD_DIM))
    angles = positions.astype(jnp.float32)[:, None] * frequency[None, :]
    cosine = jnp.cos(angles)
    sine = jnp.sin(angles)
    return jnp.concatenate([cosine, cosine], -1), jnp.concatenate([-sine, sine], -1)


def run_copies(copies):
    for copy in copies:
        copy.start()
    for copy in copies:
        copy.wait()


def core_columns(where, weight):
    half = weight.shape[1] // 2
    return pl.ds(pl.multiple_of(where[0] * half, HEAD_DIM), half)


def cut_kernel(flips, where, key_ref, value_ref, *refs):
    outs, sem = refs[:-1], refs[-1]
    columns = core_columns(where, key_ref)
    copies = []
    for out, flip in zip(outs, flips):
        size, width = out.shape
        first = 0 if flip is None else pl.multiple_of((where[1] ^ flip) * size, 16)
        for side, weight in enumerate((key_ref, value_ref)):
            target = out.at[:, side * (width // 2) : (side + 1) * (width // 2)]
            copies.append(pltpu.make_async_copy(weight.at[pl.ds(first, size), columns], target, sem.at[len(copies)]))
    run_copies(copies)


def cut_weights(where, flips, size, w_key, w_value):
    return kernel_call(
        functools.partial(cut_kernel, flips),
        "cut_weights",
        [bf16(size, w_key.shape[1])] * len(flips),
        [IN_SMEM, IN_PLACE, IN_PLACE],
        [IN_VMEM] * len(flips),
        [pltpu.SemaphoreType.DMA((2 * len(flips),))],
        limit=WIDE_LIMIT,
    )(where, w_key, w_value)


def fetch(segments, where, rows, refs, rows_held, held, sem):
    refs = list(refs)
    place = number = 0
    waits = []
    for pieces in segments:
        copies = []
        start_at = place
        for shard_flip, chip_flip, depth, size, as_given in pieces:
            first = 0 if shard_flip is None else (where[2] ^ shard_flip) * depth
            if chip_flip is not None:
                first = first + (where[1] ^ chip_flip) * size
            columns = pl.ds(first if isinstance(first, int) else pl.multiple_of(first, HEAD_DIM), size)
            into = slice(place, place + size)
            low = 0
            for part in rows:
                copies.append((part.at[:, columns], rows_held.at[low : low + part.shape[0], into]))
                low += part.shape[0]
            if as_given:
                for side in range(2):
                    weight = refs.pop(0)
                    half = weight.shape[1] // 2
                    target = held.at[into, side * half : (side + 1) * half]
                    copies.append((weight.at[:, core_columns(where, weight)], target))
            else:
                copies.append((refs.pop(0), held.at[into, :]))
            place += size
        copies = [pltpu.make_async_copy(a, b, sem.at[number + i]) for i, (a, b) in enumerate(copies)]
        number += len(copies)
        for copy in copies:
            copy.start()
        waits.append((copies, slice(start_at, place)))
    return waits


def products(waits, rows_held, held, total):
    for copies, into in waits:
        for copy in copies:
            copy.wait()
        term = jnp.dot(rows_held[:, into], held[into, :], preferred_element_type=jnp.float32)
        total = term if total is None else total + term
    return total


def partial_kernel(segments, count, where, states, other, masks, *refs):
    total_ref, rows_held, held, sem = refs[count:]
    waits = fetch(segments, where, (states, other, masks), refs[:count], rows_held, held, sem)
    total_ref[...] = products(waits, rows_held, held, None)


def finish_kernel(segments, count, has_total, where, states, other, masks, *refs):
    pieces, refs = refs[:count], refs[count:]
    total_ref = refs[0] if has_total else None
    cos_ref, sin_ref, marks_a, marks_b, *outs = refs[int(has_total) :]
    *outs, rows_held, held, kept, sem, out_sem = outs
    waits = fetch(segments, where, (states, other, masks), pieces, rows_held, held, sem)
    tokens = other.shape[0]
    masked = [jnp.broadcast_to(m[...].astype(jnp.float32), (HEAD_DIM, tokens)).T > 0.5 for m in (marks_a, marks_b)]
    sums = products(waits, rows_held, held, None if total_ref is None else total_ref[...])
    kv_heads = sums.shape[1] // 2 // HEAD_DIM
    mask_sums = sums[2 * tokens : 2 * tokens + 1]
    for head in range(kv_heads):
        for side in range(2):
            mine = slice(side * tokens, (side + 1) * tokens)
            for is_value in range(2):
                first = (is_value * kv_heads + head) * HEAD_DIM
                clean = sums[mine, first : first + HEAD_DIM]
                noisy = jnp.where(masked[side], mask_sums[:, first : first + HEAD_DIM], clean)
                for copy, part in enumerate((clean, noisy)):
                    if not is_value:
                        part = part * cos_ref[mine, :] + pltpu.roll(part, HEAD_DIM // 2, 1) * sin_ref[mine, :]
                    place = 2 * head + is_value
                    kept[copy, mine, place * HEAD_DIM : (place + 1) * HEAD_DIM] = part.astype(jnp.bfloat16)
    run_copies([pltpu.make_async_copy(kept.at[copy], outs[copy], out_sem.at[copy]) for copy in range(2)])


def project(rows, segments, where, total=None, ending=None):
    kinds, pieces = [], []
    copies = 0
    for segment in segments:
        kinds.append([])
        for piece, shard_flip, chip_flip, depth in segment:
            as_given = isinstance(piece, tuple)
            pieces.extend(piece if as_given else (piece,))
            kinds[-1].append((shard_flip, chip_flip, depth, pieces[-1].shape[0], as_given))
            copies += 5 if as_given else 4
    width = pieces[0].shape[1]
    height = sum(r.shape[0] for r in rows)
    tokens = rows[0].shape[0]
    inner = sum(kind[3] for segment in kinds for kind in segment)
    held = [
        pltpu.VMEM((height, inner), jnp.bfloat16),
        pltpu.VMEM((inner, width), jnp.bfloat16),
    ]
    sems = pltpu.SemaphoreType.DMA((copies,))
    flops = 2 * width * inner * height
    specs = [IN_SMEM] + [IN_PLACE] * (3 + len(pieces))
    if ending is None:
        return kernel_call(
            functools.partial(partial_kernel, kinds, len(pieces)),
            "project_partial",
            f32(height, width),
            specs,
            IN_VMEM,
            [*held, sems],
            flops=flops,
        )(where, *rows, *pieces)
    extra = [*(() if total is None else (total,)), *ending]
    return kernel_call(
        functools.partial(finish_kernel, kinds, len(pieces), total is not None),
        "project_finish",
        [bf16(2 * tokens, width)] * 2,
        specs + [IN_VMEM] * len(extra),
        [IN_PLACE] * 2,
        [*held, pltpu.VMEM((2, 2 * tokens, width), jnp.bfloat16), sems, pltpu.SemaphoreType.DMA((2,))],
        flops=flops,
    )(where, *rows, *pieces, *extra)


def scores_of(query, key):
    return lax.dot_general(query, key, (((1,), (1,)), ((), ())), preferred_element_type=jnp.float32)


def lane_tiles(array):
    return [array[:, lane : lane + HEAD_DIM] for lane in range(0, array.shape[1], HEAD_DIM)]


def absorb(scores, values, before):
    tiles = [lane_tiles(s) for s in scores]
    peak = functools.reduce(jnp.maximum, [t for part in tiles for t in part])
    top = jnp.broadcast_to(jnp.max(peak, -1, keepdims=True), peak.shape) * SCORE_SCALE
    if before is not None:
        top = jnp.maximum(top, before[0])
    total = mixture = None
    for part, value in zip(tiles, values):
        weights = [jnp.exp2(t * SCORE_SCALE - top) for t in part]
        for weight in weights:
            total = weight if total is None else total + weight
        mixed = jnp.dot(
            jnp.concatenate([w.astype(jnp.bfloat16) for w in weights], 1), value, preferred_element_type=jnp.float32
        )
        mixture = mixed if mixture is None else mixture + mixed
    if before is not None:
        rescale = jnp.exp2(before[0] - top)
        total = before[1] * rescale + total
        mixture = before[2] * rescale + mixture
    return top, total, mixture


def pipelined(tasks, score, use):
    waiting = None
    for task in tasks:
        scores = score(task)
        if waiting is not None:
            use(*waiting)
        waiting = (task, scores)
    use(*waiting)


def query_of(query_ref, core, head):
    first = core * (query_ref.shape[1] // 2) + head * HEAD_DIM
    return query_ref[:, pl.ds(pl.multiple_of(first, HEAD_DIM), HEAD_DIM)]


def kv_lanes(groups, head, is_value):
    first = (2 * (head // groups) + is_value) * HEAD_DIM
    return slice(first, first + HEAD_DIM)


def own_kernel(groups, where, q_a, q_b, clean_in, noisy_in, *refs):
    *state, clean_ref, noisy_ref, sem = refs
    core = where[0]
    tokens = q_a.shape[0]
    heads = state[0].shape[0]
    run_copies(
        [
            pltpu.make_async_copy(noisy_in, noisy_ref, sem.at[0]),
            pltpu.make_async_copy(clean_in, clean_ref, sem.at[1]),
        ]
    )

    def rows_of(side, ref, head, is_value):
        return ref[side * tokens : (side + 1) * tokens, kv_lanes(groups, head, is_value)]

    def score(task):
        head, side = task
        query = query_of((q_a, q_b)[side], core, head)
        near = scores_of(query, rows_of(side, noisy_ref, head, 0))
        far = scores_of(query, rows_of(1 - side, clean_ref, head, 0))
        return [near, jnp.where(core == 1 - side, far, -1e30)]

    def use(task, scores):
        head, side = task
        values = [rows_of(side, noisy_ref, head, 1), rows_of(1 - side, clean_ref, head, 1)]
        mine = pl.ds(side * tokens, tokens)
        for ref, value in zip(state, absorb(scores, values, None)):
            ref[head, mine, :] = value

    pipelined([(head, side) for head in range(heads) for side in range(2)], score, use)


def attend_own(where, queries, clean, noisy, heads, groups):
    tokens = queries[0].shape[0]
    return kernel_call(
        functools.partial(own_kernel, groups),
        "attend_own",
        [f32(heads, 2 * tokens, HEAD_DIM)] * 3,
        [IN_SMEM] + [IN_VMEM] * 2 + [IN_PLACE] * 2,
        [IN_VMEM] * 3,
        [pltpu.VMEM(clean.shape, jnp.bfloat16)] * 2 + [pltpu.SemaphoreType.DMA((2,))],
        flops=16 * heads * tokens * tokens * HEAD_DIM,
    )(where, *queries, clean, noisy)


def later_tasks(core, heads, groups, q_a, q_b, parts, state, store):
    tokens = q_a.shape[0]

    def score(task):
        head, side = task
        query = query_of((q_a, q_b)[side], core, head)
        return [scores_of(query, part[:, kv_lanes(groups, head, 0)]) for part in parts]

    def use(task, scores):
        head, side = task
        before = state(head, pl.ds(side * tokens, tokens))
        store(head, side, absorb(scores, [part[:, kv_lanes(groups, head, 1)] for part in parts], before))

    pipelined([(head, side) for head in heads for side in range(2)], score, use)


def is_earlier(where, flip):
    return (where[1] ^ flip) < where[1]


def later_kernel(groups, flips, where, q_a, q_b, *refs):
    count = len(flips)
    parts, outs = refs[:count], refs[count + 3 :]
    tokens = q_a.shape[0]

    def state(head, mine):
        return tuple(out[head, mine, :] for out in outs)

    def store(head, side, values):
        for out, value in zip(outs, values):
            out[head, pl.ds(side * tokens, tokens), :] = value

    for chosen in range(1, 1 << count):
        wanted = [bool(chosen >> number & 1) for number in range(count)]
        hits = [is_earlier(where, flip) if want else ~is_earlier(where, flip) for flip, want in zip(flips, wanted)]

        @pl.when(functools.reduce(jnp.logical_and, hits))
        def _(used=[part for part, want in zip(parts, wanted) if want]):
            later_tasks(where[0], range(outs[0].shape[0]), groups, q_a, q_b, used, state, store)


def attend_later(where, queries, parts, flips, running, groups):
    tokens = queries[0].shape[0]
    heads = running[0].shape[0]
    count = len(parts)
    return kernel_call(
        functools.partial(later_kernel, groups, flips),
        "attend_later",
        [f32(heads, 2 * tokens, HEAD_DIM)] * 3,
        [IN_SMEM] + [IN_VMEM] * (5 + count),
        [IN_VMEM] * 3,
        aliases={3 + count + i: i for i in range(3)},
        flops=8 * heads * tokens * sum(p.shape[0] for p in parts) * HEAD_DIM,
    )(where, *queries, *parts, *running)


def last_kernel(heads, groups, count, flip, where, q_a, q_b, *refs):
    parts, state_refs, outs = refs[:count], refs[count : count + 3], refs[count + 3 :]
    tokens = q_a.shape[0]

    def state(head, mine):
        return tuple(ref[head, mine, :] for ref in state_refs)

    def store(head, side, values):
        _, total, mixture = values
        total = jnp.sum(total, -1, keepdims=True)
        place = (head - heads[0]) * HEAD_DIM
        outs[side][:, place : place + HEAD_DIM] = (mixture / total).astype(jnp.bfloat16)

    @pl.when(is_earlier(where, flip))
    def _():
        later_tasks(where[0], heads, groups, q_a, q_b, parts, state, store)

    @pl.when(~is_earlier(where, flip))
    def _():
        for head in heads:
            for side in range(2):
                store(head, side, state(head, pl.ds(side * tokens, tokens)))


def attend_last(where, queries, parts, flip, running, heads, groups):
    tokens = queries[0].shape[0]
    count = len(parts)
    return kernel_call(
        functools.partial(last_kernel, heads, groups, count, flip),
        "attend_last",
        [bf16(tokens, len(heads) * HEAD_DIM)] * 2,
        [IN_SMEM] + [IN_VMEM] * (5 + count),
        [IN_VMEM] * 2,
        flops=8 * len(heads) * tokens * sum(p.shape[0] for p in parts) * HEAD_DIM,
    )(where, *queries, *parts, *running)


def place_kernel(count, where, *refs):
    parts, out, sem = refs[: 2 * count], refs[2 * count], refs[2 * count + 1]
    core = where[0]
    half = out.shape[1] // 2
    width = half // count
    copies = []
    for number, part in enumerate(parts):
        side = core if number < count else 1 - core
        first = pl.multiple_of(side * half + (number % count) * width, HEAD_DIM)
        copies.append(pltpu.make_async_copy(part, out.at[:, pl.ds(first, width)], sem.at[number]))
    for copy in copies:
        copy.start()
    for copy in copies:
        copy.wait()


def place_heads(where, mine, received):
    count = len(mine)
    tokens, width = mine[0].shape
    return kernel_call(
        functools.partial(place_kernel, count),
        "place_heads",
        bf16(tokens, 2 * count * width),
        [IN_SMEM] + [IN_VMEM] * (2 * count),
        IN_PLACE,
        [pltpu.SemaphoreType.DMA((2 * count,))],
    )(where, *mine, *received)


def as_scalars(values):
    return jnp.stack([jnp.asarray(v, jnp.int32) for v in values])


def shards(seq_size, fsdp_size, clean_states, noise_mask, mask_embed, queries, w_key, w_value):
    chips = seq_size // 2
    place = lax.axis_index("seq")
    core = lax.rem(place, 2)
    chip = place // 2
    shard = lax.axis_index("fsdp")
    states = clean_states[0]
    marks = noise_mask
    tokens = states.shape[0]
    depth, kv_width = w_key.shape
    kv_heads = kv_width // 2 // HEAD_DIM

    def swap_cores(array):
        return lax.ppermute(array, "seq", [(s, s ^ 1) for s in range(seq_size)])

    def to_chip(array, flip, sources=None):
        sources = range(chips) if sources is None else sources
        pairs = [(2 * s + c, 2 * (s ^ flip) + c) for s in sources for c in range(2)]
        return lax.ppermute(array, "seq", pairs)

    def to_shard(array, flip):
        return lax.ppermute(array, "fsdp", [(s, s ^ flip) for s in range(fsdp_size)])

    square = chips == CHIPS and fsdp_size == 4
    barrier = lax.optimization_barrier
    where = as_scalars([core, chip, shard])
    query_own = queries[0]
    if square:
        quarter = depth // chips
        (mine,) = cut_weights(where, (0,), quarter, w_key, w_value)
        far, near = to_shard(mine, 3), to_shard(mine, 1)

    mask_rows = jnp.broadcast_to(mask_embed[None, :], (MASK_ROWS, mask_embed.shape[0]))
    rows = (states, swap_cores(states), mask_rows)
    query_rows = (query_own, swap_cores(query_own))
    both_marks = (marks, swap_cores(marks))
    steps = jnp.arange(tokens, dtype=jnp.int32)
    cosine, sine = rotation(jnp.concatenate([place * tokens + steps, (place ^ 1) * tokens + steps]))

    if square:
        (corner,) = cut_weights(where, (3,), quarter, w_key, w_value)
        far, near, mine, corner, rows, query_rows, both_marks, cosine, sine = barrier(
            (far, near, mine, corner, rows, query_rows, both_marks, cosine, sine)
        )
        middle = to_shard(mine, 2)
        near_x, far_x = to_chip(near, 1), to_chip(far, 1)
        near_y, far_y = to_chip(near, 2), to_chip(far, 2)
        middle, corner, near_x, near_y, far_x, far_y = barrier((middle, corner, near_x, near_y, far_x, far_y))
        last = [to_chip(middle, flip) for flip in (3, 1, 2)]
        far_corner, near_corner = to_shard(corner, 3), to_shard(corner, 1)
        segments = [
            [((w_key, w_value), 0, None, depth)],
            [
                (far, 3, 0, depth),
                (far_x, 3, 1, depth),
                (far_y, 3, 2, depth),
            ],
            [(near, 1, 0, depth), (near_x, 1, 1, depth), (near_y, 1, 2, depth)],
        ]
        final = [
            [
                (middle, 2, 0, depth),
                (last[0], 2, 3, depth),
                (last[1], 2, 1, depth),
                (last[2], 2, 2, depth),
                (near_corner, 1, 3, depth),
                (far_corner, 3, 3, depth),
            ]
        ]
        total = project(rows, segments, where)
    else:
        (half_weights,) = cut_weights(where, (None,), depth, w_key, w_value)
        gathered = lax.all_gather(half_weights, "fsdp", axis=0, tiled=True)
        final, total = [[(gathered, None, None, depth)]], None
    clean, noisy = project(rows, final, where, total, (cosine, sine, *both_marks))

    heads = query_own.shape[1] // 2 // HEAD_DIM
    groups = heads // kv_heads
    if square:
        along_x = to_chip(clean, 1, (0, 1, 2))
        along_y = to_chip(clean, 2, (0, 1))
        running = attend_own(where, query_rows, clean, noisy, heads, groups)
        along_x, along_y, running = barrier((along_x, along_y, running))
        last_parts = [to_chip(along_x[:tokens], 2, (0, 1)), to_chip(along_y[tokens:], 1, (2, 3))]
        running = attend_later(where, query_rows, [along_x, along_y], (1, 2), running, groups)
    else:
        running = attend_own(where, query_rows, clean, noisy, heads, groups)
        for flip in range(1, chips):
            part = to_chip(clean, flip, [s for s in range(chips) if s < s ^ flip])
            if flip < chips - 1:
                running = attend_later(where, query_rows, [part], (flip,), running, groups)
        last_parts = [part]
    kept, received = [], []
    for first in range(0, heads, groups):
        own, other = attend_last(
            where, query_rows, last_parts, chips - 1, running, range(first, first + groups), groups
        )
        kept.append(own)
        received.append(swap_cores(other))
    return place_heads(where, kept, received)[None]


def solution(mesh):
    placed = (
        P("fsdp", "seq", None),
        P("fsdp", "seq"),
        P(),
        P("fsdp", "seq", None),
        P("fsdp", None),
        P("fsdp", None),
    )
    return jax.shard_map(
        functools.partial(shards, mesh.shape["seq"], mesh.shape["fsdp"]),
        mesh=mesh,
        in_specs=placed,
        out_specs=P("fsdp", "seq", None),
        check_vma=False,
    )
```

```python
import functools
import math

import jax
import jax.numpy as jnp
from jax import lax
from jax.experimental import pallas as pl
from jax.experimental.pallas import tpu as pltpu
from jax.sharding import PartitionSpec as P

HEADS = 16
HEAD_DIM = 128
BLOCK = 256
ROPE_BASE = 500000.0
MASK_ROWS = 16
CHIPS = 4
SCORE_SCALE = HEAD_DIM**-0.5 * math.log2(math.e)
VMEM_LIMIT = 16 * 1024 * 1024
WIDE_LIMIT = 56 * 1024 * 1024

IN_VMEM = pl.BlockSpec(memory_space=pltpu.VMEM)
IN_SMEM = pl.BlockSpec(memory_space=pltpu.SMEM)
IN_PLACE = pl.BlockSpec(memory_space=pl.ANY)


def kernel_call(body, name, out_shape, in_specs, out_specs, scratch=(), aliases=None, flops=0, limit=VMEM_LIMIT):
    return pl.pallas_call(
        body,
        out_shape=out_shape,
        in_specs=in_specs,
        out_specs=out_specs,
        scratch_shapes=scratch,
        input_output_aliases=aliases or {},
        compiler_params=pltpu.CompilerParams(vmem_limit_bytes=limit),
        cost_estimate=pl.CostEstimate(flops=flops, bytes_accessed=0, transcendentals=0),
        name=name,
    )


def bf16(*shape):
    return jax.ShapeDtypeStruct(shape, jnp.bfloat16)


def f32(*shape):
    return jax.ShapeDtypeStruct(shape, jnp.float32)


def rotation(positions):
    half_dim = HEAD_DIM // 2
    frequency = ROPE_BASE ** (-(jnp.arange(half_dim, dtype=jnp.float32) * 2.0 / HEAD_DIM))
    angles = positions.astype(jnp.float32)[:, None] * frequency[None, :]
    cosine = jnp.cos(angles)
    sine = jnp.sin(angles)
    return jnp.concatenate([cosine, cosine], -1), jnp.concatenate([-sine, sine], -1)


def run_copies(copies):
    for copy in copies:
        copy.start()
    for copy in copies:
        copy.wait()


def core_columns(where, weight):
    half = weight.shape[1] // 2
    return pl.ds(pl.multiple_of(where[0] * half, HEAD_DIM), half)


def cut_kernel(flips, where, key_ref, value_ref, *refs):
    outs, sem = refs[:-1], refs[-1]
    columns = core_columns(where, key_ref)
    copies = []
    for out, flip in zip(outs, flips):
        size, width = out.shape
        first = 0 if flip is None else pl.multiple_of((where[1] ^ flip) * size, 16)
        for side, weight in enumerate((key_ref, value_ref)):
            target = out.at[:, side * (width // 2) : (side + 1) * (width // 2)]
            copies.append(pltpu.make_async_copy(weight.at[pl.ds(first, size), columns], target, sem.at[len(copies)]))
    run_copies(copies)


def cut_weights(where, flips, size, w_key, w_value):
    return kernel_call(
        functools.partial(cut_kernel, flips),
        "cut_weights",
        [bf16(size, w_key.shape[1])] * len(flips),
        [IN_SMEM, IN_PLACE, IN_PLACE],
        [IN_VMEM] * len(flips),
        [pltpu.SemaphoreType.DMA((2 * len(flips),))],
        limit=WIDE_LIMIT,
    )(where, w_key, w_value)


def fetch(segments, where, rows, refs, rows_held, held, sem):
    refs = list(refs)
    place = number = 0
    waits = []
    for pieces in segments:
        copies = []
        start_at = place
        for shard_flip, chip_flip, depth, size, as_given in pieces:
            first = 0 if shard_flip is None else (where[2] ^ shard_flip) * depth
            if chip_flip is not None:
                first = first + (where[1] ^ chip_flip) * size
            columns = pl.ds(first if isinstance(first, int) else pl.multiple_of(first, HEAD_DIM), size)
            into = slice(place, place + size)
            low = 0
            for part in rows:
                copies.append((part.at[:, columns], rows_held.at[low : low + part.shape[0], into]))
                low += part.shape[0]
            if held is None:
                pass
            elif as_given:
                for side in range(2):
                    weight = refs.pop(0)
                    half = weight.shape[1] // 2
                    target = held.at[into, side * half : (side + 1) * half]
                    copies.append((weight.at[:, core_columns(where, weight)], target))
            else:
                copies.append((refs.pop(0), held.at[into, :]))
            place += size
        copies = [pltpu.make_async_copy(a, b, sem.at[number + i]) for i, (a, b) in enumerate(copies)]
        number += len(copies)
        for copy in copies:
            copy.start()
        waits.append((copies, slice(start_at, place)))
    return waits


def products(waits, rows_held, held, total):
    for copies, into in waits:
        for copy in copies:
            copy.wait()
        term = jnp.dot(rows_held[:, into], held[into, :], preferred_element_type=jnp.float32)
        total = term if total is None else total + term
    return total


def partial_kernel(segments, final, count, where, states, other, masks, *refs):
    total_ref, final_rows, rows_held, held, sem, final_sem = refs[count:]
    rows = (states, other, masks)
    waits = fetch(segments, where, rows, refs[:count], rows_held, held, sem)
    final_waits = fetch(final, where, rows, (), final_rows, None, final_sem)
    total_ref[...] = products(waits, rows_held, held, None)
    for copies, _ in final_waits:
        for copy in copies:
            copy.wait()


def rotated(key, cosine, sine):
    return key * cosine + pltpu.roll(key, HEAD_DIM // 2, 1) * sine


def finish_kernel(segments, count, staged, tokens, where, *refs):
    if staged:
        total_ref, rows_held = refs[:2]
        rows, total, refs = (), total_ref[...], refs[2:]
    else:
        rows, total, refs = refs[:3], None, refs[3:]
    pieces, (cos_ref, sin_ref, *refs) = refs[:count], refs[count:]
    clean_out, mask_out, refs = refs[0], refs[1], refs[2:]
    if not staged:
        rows_held, *refs = refs
    held, kept, sem, out_sem = refs
    waits = fetch(segments, where, rows, pieces, rows_held, held, sem)
    sums = products(waits, rows_held, held, total)
    kv_heads = sums.shape[1] // 2 // HEAD_DIM
    writes = []
    for side in range(2):
        mine = slice(side * tokens, (side + 1) * tokens)
        for head in range(kv_heads):
            for is_value in range(2):
                first = (is_value * kv_heads + head) * HEAD_DIM
                part = sums[mine, first : first + HEAD_DIM]
                if not is_value:
                    part = rotated(part, cos_ref[mine, :], sin_ref[mine, :])
                place = (2 * head + is_value) * HEAD_DIM
                kept[side, :, place : place + HEAD_DIM] = part.astype(jnp.bfloat16)
        writes.append(pltpu.make_async_copy(kept.at[side], clean_out.at[mine, :], out_sem.at[side]))
        writes[-1].start()
    mask_out[...] = sums[2 * tokens : 2 * tokens + 8]
    for write in writes:
        write.wait()


def describe(segments):
    kinds, arrays, copies = [], [], 0
    for segment in segments:
        kinds.append([])
        for piece, shard_flip, chip_flip, depth in segment:
            as_given = isinstance(piece, tuple)
            arrays.extend(piece if as_given else (piece,))
            kinds[-1].append((shard_flip, chip_flip, depth, arrays[-1].shape[0], as_given))
            copies += 5 if as_given else 4
    return kinds, arrays, sum(kind[3] for segment in kinds for kind in segment), copies


def project_partial(rows, segments, final, where):
    kinds, arrays, inner, copies = describe(segments)
    final_kinds, _, final_inner, final_copies = describe(final)
    width = arrays[0].shape[1]
    height = sum(r.shape[0] for r in rows)
    return kernel_call(
        functools.partial(partial_kernel, kinds, final_kinds, len(arrays)),
        "project_partial",
        [f32(height, width), bf16(height, final_inner)],
        [IN_SMEM] + [IN_PLACE] * (3 + len(arrays)),
        [IN_VMEM] * 2,
        [
            pltpu.VMEM((height, inner), jnp.bfloat16),
            pltpu.VMEM((inner, width), jnp.bfloat16),
            pltpu.SemaphoreType.DMA((copies,)),
            pltpu.SemaphoreType.DMA((final_copies,)),
        ],
        flops=2 * width * inner * height,
    )(where, *rows, *arrays)


def project_finish(rows, staged, segments, where, ending):
    kinds, arrays, inner, copies = describe(segments)
    width = arrays[0].shape[1]
    tokens = rows[0].shape[0]
    height = sum(r.shape[0] for r in rows)
    scratch = [] if staged else [pltpu.VMEM((height, inner), jnp.bfloat16)]
    begin = staged or rows
    return kernel_call(
        functools.partial(finish_kernel, kinds, len(arrays), bool(staged), tokens),
        "project_finish",
        [bf16(2 * tokens, width), f32(8, width)],
        [IN_SMEM] + [IN_VMEM if staged else IN_PLACE] * len(begin) + [IN_PLACE] * len(arrays) + [IN_VMEM] * len(ending),
        [IN_PLACE, IN_VMEM],
        [
            *scratch,
            pltpu.VMEM((inner, width), jnp.bfloat16),
            pltpu.VMEM((2, tokens, width), jnp.bfloat16),
            pltpu.SemaphoreType.DMA((copies,)),
            pltpu.SemaphoreType.DMA((2,)),
        ],
        flops=2 * width * inner * height,
    )(where, *begin, *arrays, *ending)


def scores_of(query, key):
    return lax.dot_general(query, key, (((1,), (1,)), ((), ())), preferred_element_type=jnp.float32)


def lane_tiles(array):
    return [array[:, lane : lane + HEAD_DIM] for lane in range(0, array.shape[1], HEAD_DIM)]


def absorb(scores, values, before):
    tiles = [lane_tiles(s) for s in scores]
    peak = functools.reduce(jnp.maximum, [t for part in tiles for t in part])
    top = jnp.broadcast_to(jnp.max(peak, -1, keepdims=True), peak.shape) * SCORE_SCALE
    if before is not None:
        top = jnp.maximum(top, before[0])
    both = None
    for part, value in zip(tiles, values):
        weights = jnp.concatenate([jnp.exp2(t * SCORE_SCALE - top).astype(jnp.bfloat16) for t in part], 1)
        wide = jnp.concatenate([value, jnp.ones_like(value)], 1)
        term = jnp.dot(weights, wide, preferred_element_type=jnp.float32)
        both = term if both is None else both + term
    mixture, total = both[:, :HEAD_DIM], both[:, HEAD_DIM:]
    if before is not None:
        rescale = jnp.exp2(before[0] - top)
        total = before[1] * rescale + total
        mixture = before[2] * rescale + mixture
    return top, total, mixture


def pipelined(tasks, score, use):
    waiting = None
    for task in tasks:
        scores = score(task)
        if waiting is not None:
            use(*waiting)
        waiting = (task, scores)
    use(*waiting)


def query_of(query_ref, core, head):
    first = core * (query_ref.shape[1] // 2) + head * HEAD_DIM
    return query_ref[:, pl.ds(pl.multiple_of(first, HEAD_DIM), HEAD_DIM)]


def kv_lanes(groups, head, is_value):
    first = (2 * (head // groups) + is_value) * HEAD_DIM
    return slice(first, first + HEAD_DIM)


def own_kernel(groups, where, q_a, q_b, cos_ref, sin_ref, marks_a, marks_b, mask_ref, *refs):
    clean_in, state, (clean_ref, noisy_ref, sem) = refs[0], refs[1:4], refs[4:]
    core = where[0]
    tokens = q_a.shape[0]
    heads = state[0].shape[0]
    run_copies(
        [
            pltpu.make_async_copy(clean_in.at[i * tokens : (i + 1) * tokens, :], clean_ref.at[i], sem.at[i])
            for i in range(2)
        ]
    )
    for side, marks in enumerate((marks_a, marks_b)):
        mine = slice(side * tokens, (side + 1) * tokens)
        masked = jnp.broadcast_to(marks[...].astype(jnp.float32), (HEAD_DIM, tokens)).T > 0.5
        for head in range(heads // groups):
            for is_value in range(2):
                first = (is_value * (heads // groups) + head) * HEAD_DIM
                token = jnp.broadcast_to(mask_ref[:1, first : first + HEAD_DIM], (tokens, HEAD_DIM))
                if not is_value:
                    token = rotated(token, cos_ref[mine, :], sin_ref[mine, :])
                lanes = kv_lanes(groups, head * groups, is_value)
                clean = clean_ref[side, :, lanes].astype(jnp.float32)
                noisy_ref[side, :, lanes] = jnp.where(masked, token, clean).astype(jnp.bfloat16)

    def score(task):
        head, side = task
        query = query_of((q_a, q_b)[side], core, head)
        lanes = kv_lanes(groups, head, 0)
        near = scores_of(query, noisy_ref[side, :, lanes])
        far = scores_of(query, clean_ref[1 - side, :, lanes])
        return [near, jnp.where(core == 1 - side, far, -1e30)]

    def use(task, scores):
        head, side = task
        lanes = kv_lanes(groups, head, 1)
        values = [noisy_ref[side, :, lanes], clean_ref[1 - side, :, lanes]]
        mine = pl.ds(side * tokens, tokens)
        for ref, value in zip(state, absorb(scores, values, None)):
            ref[head, mine, :] = value

    pipelined([(head, side) for head in range(heads) for side in range(2)], score, use)


def attend_own(where, queries, tables, marks, mask_sums, clean, heads, groups):
    tokens = queries[0].shape[0]
    return kernel_call(
        functools.partial(own_kernel, groups),
        "attend_own",
        [f32(heads, 2 * tokens, HEAD_DIM)] * 3,
        [IN_SMEM] + [IN_VMEM] * 7 + [IN_PLACE],
        [IN_VMEM] * 3,
        [pltpu.VMEM((2, tokens, clean.shape[1]), jnp.bfloat16)] * 2 + [pltpu.SemaphoreType.DMA((2,))],
        flops=16 * heads * tokens * tokens * HEAD_DIM,
    )(where, *queries, *tables, *marks, mask_sums, clean)


def later_tasks(core, heads, groups, q_a, q_b, parts, state, store):
    def score(head):
        query = jnp.concatenate([query_of(q, core, head) for q in (q_a, q_b)], 0)
        return [scores_of(query, part[:, kv_lanes(groups, head, 0)]) for part in parts]

    def use(head, scores):
        store(head, absorb(scores, [part[:, kv_lanes(groups, head, 1)] for part in parts], state(head)))

    pipelined(heads, score, use)


def is_earlier(where, flip):
    return (where[1] ^ flip) < where[1]


def later_kernel(groups, flips, where, q_a, q_b, *refs):
    count = len(flips)
    parts, outs = refs[:count], refs[count + 3 :]

    def state(head):
        return tuple(out[head] for out in outs)

    def store(head, values):
        for out, value in zip(outs, values):
            out[head] = value

    chips = sorted(set(flips))
    for chosen in range(1, 1 << len(chips)):
        wanted = [flip for number, flip in enumerate(chips) if chosen >> number & 1]
        hits = [is_earlier(where, flip) if flip in wanted else ~is_earlier(where, flip) for flip in chips]

        @pl.when(functools.reduce(jnp.logical_and, hits))
        def _(used=[part for part, flip in zip(parts, flips) if flip in wanted]):
            later_tasks(where[0], range(outs[0].shape[0]), groups, q_a, q_b, used, state, store)


def attend_later(where, queries, parts, flips, running, groups):
    tokens = queries[0].shape[0]
    heads = running[0].shape[0]
    count = len(parts)
    return kernel_call(
        functools.partial(later_kernel, groups, flips),
        "attend_later",
        [f32(heads, 2 * tokens, HEAD_DIM)] * 3,
        [IN_SMEM] + [IN_VMEM] * (5 + count),
        [IN_VMEM] * 3,
        aliases={3 + count + i: i for i in range(3)},
        flops=8 * heads * tokens * sum(p.shape[0] for p in parts) * HEAD_DIM,
    )(where, *queries, *parts, *running)


def last_kernel(heads, groups, count, flip, where, q_a, q_b, *refs):
    parts, state_refs, outs = refs[:count], refs[count : count + 3], refs[count + 3 :]
    tokens = q_a.shape[0]

    def state(head):
        return tuple(ref[head] for ref in state_refs)

    def store(head, values):
        _, total, mixture = values
        result = (mixture / total).astype(jnp.bfloat16)
        place = (head - heads[0]) * HEAD_DIM
        for side, out in enumerate(outs):
            out[:, place : place + HEAD_DIM] = result[side * tokens : (side + 1) * tokens]

    @pl.when(is_earlier(where, flip))
    def _():
        later_tasks(where[0], heads, groups, q_a, q_b, parts, state, store)

    @pl.when(~is_earlier(where, flip))
    def _():
        for head in heads:
            store(head, state(head))


def attend_last(where, queries, parts, flip, running, heads, groups):
    tokens = queries[0].shape[0]
    count = len(parts)
    return kernel_call(
        functools.partial(last_kernel, heads, groups, count, flip),
        "attend_last",
        [bf16(tokens, len(heads) * HEAD_DIM)] * 2,
        [IN_SMEM] + [IN_VMEM] * (5 + count),
        [IN_VMEM] * 2,
        flops=8 * len(heads) * tokens * sum(p.shape[0] for p in parts) * HEAD_DIM,
    )(where, *queries, *parts, *running)


def place_kernel(count, where, *refs):
    parts, out, sem = refs[: 2 * count], refs[2 * count], refs[2 * count + 1]
    core = where[0]
    half = out.shape[1] // 2
    width = half // count
    copies = []
    for number, part in enumerate(parts):
        side = core if number < count else 1 - core
        first = pl.multiple_of(side * half + (number % count) * width, HEAD_DIM)
        copies.append(pltpu.make_async_copy(part, out.at[:, pl.ds(first, width)], sem.at[number]))
    for copy in copies:
        copy.start()
    for copy in copies:
        copy.wait()


def place_heads(where, mine, received):
    count = len(mine)
    tokens, width = mine[0].shape
    return kernel_call(
        functools.partial(place_kernel, count),
        "place_heads",
        bf16(tokens, 2 * count * width),
        [IN_SMEM] + [IN_VMEM] * (2 * count),
        IN_PLACE,
        [pltpu.SemaphoreType.DMA((2 * count,))],
    )(where, *mine, *received)


def as_scalars(values):
    return jnp.stack([jnp.asarray(v, jnp.int32) for v in values])


def shards(seq_size, fsdp_size, clean_states, noise_mask, mask_embed, queries, w_key, w_value):
    chips = seq_size // 2
    place = lax.axis_index("seq")
    core = lax.rem(place, 2)
    chip = place // 2
    shard = lax.axis_index("fsdp")
    states = clean_states[0]
    marks = noise_mask
    tokens = states.shape[0]
    depth, kv_width = w_key.shape
    kv_heads = kv_width // 2 // HEAD_DIM

    def swap_cores(array):
        return lax.ppermute(array, "seq", [(s, s ^ 1) for s in range(seq_size)])

    def to_chip(array, flip, sources=None):
        sources = range(chips) if sources is None else sources
        pairs = [(2 * s + c, 2 * (s ^ flip) + c) for s in sources for c in range(2)]
        return lax.ppermute(array, "seq", pairs)

    def to_shard(array, flip):
        return lax.ppermute(array, "fsdp", [(s, s ^ flip) for s in range(fsdp_size)])

    square = chips == CHIPS and fsdp_size == 4
    barrier = lax.optimization_barrier
    where = as_scalars([core, chip, shard])
    query_own = queries[0]
    if square:
        quarter = depth // chips
        half = kv_width // 2
        mine = jnp.concatenate(
            [lax.dynamic_slice(w, (chip * quarter, core * half), (quarter, half)) for w in (w_key, w_value)], 1
        )
        far, near = to_shard(mine, 3), to_shard(mine, 1)

    mask_rows = jnp.broadcast_to(mask_embed[None, :], (MASK_ROWS, mask_embed.shape[0]))
    rows = (states, swap_cores(states), mask_rows)
    query_rows = (query_own, swap_cores(query_own))
    both_marks = (marks, swap_cores(marks))
    steps = jnp.arange(tokens, dtype=jnp.int32)
    cosine, sine = rotation(jnp.concatenate([place * tokens + steps, (place ^ 1) * tokens + steps]))

    if square:
        (corner,) = cut_weights(where, (3,), quarter, w_key, w_value)
        far, near, mine, corner, rows, query_rows, both_marks, cosine, sine = barrier(
            (far, near, mine, corner, rows, query_rows, both_marks, cosine, sine)
        )
        middle = to_shard(mine, 2)
        near_x, far_x = to_chip(near, 1), to_chip(far, 1)
        near_y, far_y = to_chip(near, 2), to_chip(far, 2)
        middle, corner, near_x, near_y, far_x, far_y = barrier((middle, corner, near_x, near_y, far_x, far_y))
        far_corner, near_corner = to_shard(corner, 3), to_shard(corner, 1)
        last = [to_chip(middle, flip) for flip in (3, 1, 2)]
        segments = [
            [((w_key, w_value), 0, None, depth)],
            [
                (far, 3, 0, depth),
                (far_x, 3, 1, depth),
                (far_y, 3, 2, depth),
            ],
            [(near, 1, 0, depth), (near_x, 1, 1, depth), (near_y, 1, 2, depth)],
        ]
        final = [
            [
                (middle, 2, 0, depth),
                (last[0], 2, 3, depth),
                (last[1], 2, 1, depth),
                (last[2], 2, 2, depth),
                (near_corner, 1, 3, depth),
                (far_corner, 3, 3, depth),
            ]
        ]
        staged = project_partial(rows, segments, final, where)
    else:
        (half_weights,) = cut_weights(where, (None,), depth, w_key, w_value)
        gathered = lax.all_gather(half_weights, "fsdp", axis=0, tiled=True)
        final, staged = [[(gathered, None, None, depth)]], ()
    tables = (cosine, sine)
    clean, mask_sums = project_finish(rows, staged, final, where, tables)

    heads = query_own.shape[1] // 2 // HEAD_DIM
    groups = heads // kv_heads
    if square:
        along_x, along_y = to_chip(clean, 1, (0, 1, 2)), to_chip(clean, 2, (0, 1))
        running = attend_own(where, query_rows, tables, both_marks, mask_sums, clean, heads, groups)
        along_x, along_y, running = barrier((along_x, along_y, running))
        last_parts = [to_chip(along_x[:tokens], 2, (0, 1)), to_chip(along_y[tokens:], 1, (2, 3))]
        running = attend_later(where, query_rows, [along_x, along_y], (1, 2), running, groups)
    else:
        running = attend_own(where, query_rows, tables, both_marks, mask_sums, clean, heads, groups)
        for flip in range(1, chips):
            parts = [to_chip(clean, flip, [s for s in range(chips) if s < s ^ flip])]
            if flip < chips - 1:
                running = attend_later(where, query_rows, parts, (flip,), running, groups)
        last_parts = parts
    kept, received = [], []
    for first in range(0, heads, groups):
        own, other = attend_last(
            where, query_rows, last_parts, chips - 1, running, range(first, first + groups), groups
        )
        kept.append(own)
        received.append(swap_cores(other))
    return place_heads(where, kept, received)[None]


def solution(mesh):
    placed = (
        P("fsdp", "seq", None),
        P("fsdp", "seq"),
        P(),
        P("fsdp", "seq", None),
        P("fsdp", None),
        P("fsdp", None),
    )
    return jax.shard_map(
        functools.partial(shards, mesh.shape["seq"], mesh.shape["fsdp"]),
        mesh=mesh,
        in_specs=placed,
        out_specs=P("fsdp", "seq", None),
        check_vma=False,
    )
```

```python
import functools
import math

import jax
import jax.numpy as jnp
from jax import lax
from jax.experimental import pallas as pl
from jax.experimental.pallas import tpu as pltpu
from jax.sharding import PartitionSpec as P

HEADS = 16
HEAD_DIM = 128
BLOCK = 256
ROPE_BASE = 500000.0
MASK_ROWS = 16
CHIPS = 4
SCORE_SCALE = HEAD_DIM**-0.5 * math.log2(math.e)
VMEM_LIMIT = 16 * 1024 * 1024
WIDE_LIMIT = 56 * 1024 * 1024

IN_VMEM = pl.BlockSpec(memory_space=pltpu.VMEM)
IN_SMEM = pl.BlockSpec(memory_space=pltpu.SMEM)
IN_PLACE = pl.BlockSpec(memory_space=pl.ANY)


def kernel_call(body, name, out_shape, in_specs, out_specs, scratch=(), aliases=None, flops=0, limit=VMEM_LIMIT):
    return pl.pallas_call(
        body,
        out_shape=out_shape,
        in_specs=in_specs,
        out_specs=out_specs,
        scratch_shapes=scratch,
        input_output_aliases=aliases or {},
        compiler_params=pltpu.CompilerParams(vmem_limit_bytes=limit),
        cost_estimate=pl.CostEstimate(flops=flops, bytes_accessed=0, transcendentals=0),
        name=name,
    )


def bf16(*shape):
    return jax.ShapeDtypeStruct(shape, jnp.bfloat16)


def f32(*shape):
    return jax.ShapeDtypeStruct(shape, jnp.float32)


def rotation(positions):
    half_dim = HEAD_DIM // 2
    frequency = ROPE_BASE ** (-(jnp.arange(half_dim, dtype=jnp.float32) * 2.0 / HEAD_DIM))
    angles = positions.astype(jnp.float32)[:, None] * frequency[None, :]
    cosine = jnp.cos(angles)
    sine = jnp.sin(angles)
    return jnp.concatenate([cosine, cosine], -1), jnp.concatenate([-sine, sine], -1)


def run_copies(copies):
    for copy in copies:
        copy.start()
    for copy in copies:
        copy.wait()


def core_columns(where, weight):
    half = weight.shape[1] // 2
    return pl.ds(pl.multiple_of(where[0] * half, HEAD_DIM), half)


def cut_kernel(flips, where, key_ref, value_ref, *refs):
    outs, sem = refs[:-1], refs[-1]
    columns = core_columns(where, key_ref)
    copies = []
    for out, flip in zip(outs, flips):
        size, width = out.shape
        first = 0 if flip is None else pl.multiple_of((where[1] ^ flip) * size, 16)
        for side, weight in enumerate((key_ref, value_ref)):
            target = out.at[:, side * (width // 2) : (side + 1) * (width // 2)]
            copies.append(pltpu.make_async_copy(weight.at[pl.ds(first, size), columns], target, sem.at[len(copies)]))
    run_copies(copies)


def cut_weights(where, flips, size, w_key, w_value):
    return kernel_call(
        functools.partial(cut_kernel, flips),
        "cut_weights",
        [bf16(size, w_key.shape[1])] * len(flips),
        [IN_SMEM, IN_PLACE, IN_PLACE],
        [IN_VMEM] * len(flips),
        [pltpu.SemaphoreType.DMA((2 * len(flips),))],
        limit=WIDE_LIMIT,
    )(where, w_key, w_value)


def fetch(segments, where, rows, refs, rows_held, held, sem):
    refs = list(refs)
    place = number = 0
    waits = []
    for pieces in segments:
        copies = []
        start_at = place
        for shard_flip, chip_flip, depth, size, as_given in pieces:
            first = 0 if shard_flip is None else (where[2] ^ shard_flip) * depth
            if chip_flip is not None:
                first = first + (where[1] ^ chip_flip) * size
            columns = pl.ds(first if isinstance(first, int) else pl.multiple_of(first, HEAD_DIM), size)
            into = slice(place, place + size)
            low = 0
            for part in rows:
                copies.append((part.at[:, columns], rows_held.at[low : low + part.shape[0], into]))
                low += part.shape[0]
            if held is None:
                pass
            elif as_given:
                for side in range(2):
                    weight = refs.pop(0)
                    half = weight.shape[1] // 2
                    target = held.at[into, side * half : (side + 1) * half]
                    copies.append((weight.at[:, core_columns(where, weight)], target))
            else:
                copies.append((refs.pop(0), held.at[into, :]))
            place += size
        copies = [pltpu.make_async_copy(a, b, sem.at[number + i]) for i, (a, b) in enumerate(copies)]
        number += len(copies)
        for copy in copies:
            copy.start()
        waits.append((copies, slice(start_at, place)))
    return waits


def products(waits, rows_held, held, total):
    for copies, into in waits:
        for copy in copies:
            copy.wait()
        term = jnp.dot(rows_held[:, into], held[into, :], preferred_element_type=jnp.float32)
        total = term if total is None else total + term
    return total


def partial_kernel(segments, final, count, where, states, other, masks, *refs):
    total_ref, final_rows, rows_held, held, sem, final_sem = refs[count:]
    rows = (states, other, masks)
    waits = fetch(segments, where, rows, refs[:count], rows_held, held, sem)
    final_waits = fetch(final, where, rows, (), final_rows, None, final_sem)
    total_ref[...] = products(waits, rows_held, held, None)
    for copies, _ in final_waits:
        for copy in copies:
            copy.wait()


def rotated(key, cosine, sine):
    return key * cosine + pltpu.roll(key, HEAD_DIM // 2, 1) * sine


def finish_kernel(segments, count, staged, tokens, where, *refs):
    if staged:
        total_ref, rows_held = refs[:2]
        rows, total, refs = (), total_ref[...], refs[2:]
    else:
        rows, total, refs = refs[:3], None, refs[3:]
    pieces, (cos_ref, sin_ref, *refs) = refs[:count], refs[count:]
    clean_outs, mask_out, refs = refs[:2], refs[2], refs[3:]
    if not staged:
        rows_held, *refs = refs
    held, kept, sem, out_sem = refs
    waits = fetch(segments, where, rows, pieces, rows_held, held, sem)
    sums = products(waits, rows_held, held, total)
    kv_heads = sums.shape[1] // 2 // HEAD_DIM
    writes = []
    for is_value, out in enumerate(clean_outs):
        for head in range(kv_heads):
            lanes = slice(head * HEAD_DIM, (head + 1) * HEAD_DIM)
            first = (is_value * kv_heads + head) * HEAD_DIM
            part = sums[: 2 * tokens, first : first + HEAD_DIM]
            if not is_value:
                part = rotated(part, cos_ref[...], sin_ref[...])
            kept[is_value, :, lanes] = part.astype(jnp.bfloat16)
        writes.append(pltpu.make_async_copy(kept.at[is_value], out, out_sem.at[is_value]))
        writes[-1].start()
    mask_out[...] = sums[2 * tokens : 2 * tokens + 8]
    for write in writes:
        write.wait()


def describe(segments):
    kinds, arrays, copies = [], [], 0
    for segment in segments:
        kinds.append([])
        for piece, shard_flip, chip_flip, depth in segment:
            as_given = isinstance(piece, tuple)
            arrays.extend(piece if as_given else (piece,))
            kinds[-1].append((shard_flip, chip_flip, depth, arrays[-1].shape[0], as_given))
            copies += 5 if as_given else 4
    return kinds, arrays, sum(kind[3] for segment in kinds for kind in segment), copies


def project_partial(rows, segments, final, where):
    kinds, arrays, inner, copies = describe(segments)
    final_kinds, _, final_inner, final_copies = describe(final)
    width = arrays[0].shape[1]
    height = sum(r.shape[0] for r in rows)
    return kernel_call(
        functools.partial(partial_kernel, kinds, final_kinds, len(arrays)),
        "project_partial",
        [f32(height, width), bf16(height, final_inner)],
        [IN_SMEM] + [IN_PLACE] * (3 + len(arrays)),
        [IN_VMEM] * 2,
        [
            pltpu.VMEM((height, inner), jnp.bfloat16),
            pltpu.VMEM((inner, width), jnp.bfloat16),
            pltpu.SemaphoreType.DMA((copies,)),
            pltpu.SemaphoreType.DMA((final_copies,)),
        ],
        flops=2 * width * inner * height,
    )(where, *rows, *arrays)


def project_finish(rows, staged, segments, where, ending):
    kinds, arrays, inner, copies = describe(segments)
    width = arrays[0].shape[1]
    tokens = rows[0].shape[0]
    height = sum(r.shape[0] for r in rows)
    scratch = [] if staged else [pltpu.VMEM((height, inner), jnp.bfloat16)]
    begin = staged or rows
    return kernel_call(
        functools.partial(finish_kernel, kinds, len(arrays), bool(staged), tokens),
        "project_finish",
        [bf16(2 * tokens, width // 2)] * 2 + [f32(8, width)],
        [IN_SMEM] + [IN_VMEM if staged else IN_PLACE] * len(begin) + [IN_PLACE] * len(arrays) + [IN_VMEM] * len(ending),
        [IN_PLACE] * 2 + [IN_VMEM],
        [
            *scratch,
            pltpu.VMEM((inner, width), jnp.bfloat16),
            pltpu.VMEM((2, 2 * tokens, width // 2), jnp.bfloat16),
            pltpu.SemaphoreType.DMA((copies,)),
            pltpu.SemaphoreType.DMA((2,)),
        ],
        flops=2 * width * inner * height,
    )(where, *begin, *arrays, *ending)


def scores_of(query, key):
    return lax.dot_general(query, key, (((1,), (1,)), ((), ())), preferred_element_type=jnp.float32)


def lane_tiles(array):
    return [array[:, lane : lane + HEAD_DIM] for lane in range(0, array.shape[1], HEAD_DIM)]


def absorb(scores, values, before):
    tiles = [lane_tiles(s) for s in scores]
    peak = functools.reduce(jnp.maximum, [t for part in tiles for t in part])
    top = jnp.broadcast_to(jnp.max(peak, -1, keepdims=True), peak.shape) * SCORE_SCALE
    if before is not None:
        top = jnp.maximum(top, before[0])
    both = None
    for part, value in zip(tiles, values):
        weights = jnp.concatenate([jnp.exp2(t * SCORE_SCALE - top).astype(jnp.bfloat16) for t in part], 1)
        wide = jnp.concatenate([value, jnp.ones_like(value)], 1)
        term = jnp.dot(weights, wide, preferred_element_type=jnp.float32)
        both = term if both is None else both + term
    mixture, total = both[:, :HEAD_DIM], both[:, HEAD_DIM:]
    if before is not None:
        rescale = jnp.exp2(before[0] - top)
        total = before[1] * rescale + total
        mixture = before[2] * rescale + mixture
    return top, total, mixture


def pipelined(tasks, score, use):
    waiting = None
    for task in tasks:
        scores = score(task)
        if waiting is not None:
            use(*waiting)
        waiting = (task, scores)
    use(*waiting)


def query_of(query_ref, core, head):
    first = core * (query_ref.shape[1] // 2) + head * HEAD_DIM
    return query_ref[:, pl.ds(pl.multiple_of(first, HEAD_DIM), HEAD_DIM)]


def kv_lanes(groups, head):
    first = head // groups * HEAD_DIM
    return slice(first, first + HEAD_DIM)


def own_kernel(groups, where, q_a, q_b, cos_ref, sin_ref, marks_a, marks_b, mask_ref, *refs):
    clean_ins, state, (clean_ref, noisy_ref, sem) = refs[:2], refs[2:5], refs[5:]
    core = where[0]
    tokens = q_a.shape[0]
    heads = state[0].shape[0]
    run_copies([pltpu.make_async_copy(ref, clean_ref.at[i], sem.at[i]) for i, ref in enumerate(clean_ins)])
    for side, marks in enumerate((marks_a, marks_b)):
        mine = slice(side * tokens, (side + 1) * tokens)
        masked = jnp.broadcast_to(marks[...].astype(jnp.float32), (HEAD_DIM, tokens)).T > 0.5
        for head in range(heads // groups):
            for is_value in range(2):
                first = (is_value * (heads // groups) + head) * HEAD_DIM
                token = jnp.broadcast_to(mask_ref[:1, first : first + HEAD_DIM], (tokens, HEAD_DIM))
                if not is_value:
                    token = rotated(token, cos_ref[mine, :], sin_ref[mine, :])
                lanes = kv_lanes(groups, head * groups)
                clean = clean_ref[is_value, mine, lanes].astype(jnp.float32)
                noisy_ref[is_value, mine, lanes] = jnp.where(masked, token, clean).astype(jnp.bfloat16)

    def rows_of(ref, is_value, head, side):
        return ref[is_value, side * tokens : (side + 1) * tokens, kv_lanes(groups, head)]

    def score(task):
        head, side = task
        query = query_of((q_a, q_b)[side], core, head)
        near = scores_of(query, rows_of(noisy_ref, 0, head, side))
        far = scores_of(query, rows_of(clean_ref, 0, head, 1 - side))
        return [near, jnp.where(core == 1 - side, far, -1e30)]

    def use(task, scores):
        head, side = task
        values = [rows_of(noisy_ref, 1, head, side), rows_of(clean_ref, 1, head, 1 - side)]
        mine = pl.ds(side * tokens, tokens)
        for ref, value in zip(state, absorb(scores, values, None)):
            ref[head, mine, :] = value

    pipelined([(head, side) for head in range(heads) for side in range(2)], score, use)


def attend_own(where, queries, tables, marks, mask_sums, clean, heads, groups):
    tokens = queries[0].shape[0]
    return kernel_call(
        functools.partial(own_kernel, groups),
        "attend_own",
        [f32(heads, 2 * tokens, HEAD_DIM)] * 3,
        [IN_SMEM] + [IN_VMEM] * 7 + [IN_PLACE] * 2,
        [IN_VMEM] * 3,
        [pltpu.VMEM((2, *clean[0].shape), jnp.bfloat16)] * 2 + [pltpu.SemaphoreType.DMA((2,))],
        flops=16 * heads * tokens * tokens * HEAD_DIM,
    )(where, *queries, *tables, *marks, mask_sums, *clean)


def later_tasks(core, heads, groups, q_a, q_b, parts, state, store):
    def score(head):
        query = jnp.concatenate([query_of(q, core, head) for q in (q_a, q_b)], 0)
        return [scores_of(query, keys[:, kv_lanes(groups, head)]) for keys, _ in parts]

    def use(head, scores):
        store(head, absorb(scores, [values[:, kv_lanes(groups, head)] for _, values in parts], state(head)))

    pipelined(heads, score, use)


def pairs(refs):
    return list(zip(refs[::2], refs[1::2]))


def is_earlier(where, flip):
    return (where[1] ^ flip) < where[1]


def later_kernel(groups, flips, where, q_a, q_b, *refs):
    count = len(flips)
    parts, outs = pairs(refs[: 2 * count]), refs[2 * count + 3 :]

    def state(head):
        return tuple(out[head] for out in outs)

    def store(head, values):
        for out, value in zip(outs, values):
            out[head] = value

    chips = sorted(set(flips))
    for chosen in range(1, 1 << len(chips)):
        wanted = [flip for number, flip in enumerate(chips) if chosen >> number & 1]
        hits = [is_earlier(where, flip) if flip in wanted else ~is_earlier(where, flip) for flip in chips]

        @pl.when(functools.reduce(jnp.logical_and, hits))
        def _(used=[part for part, flip in zip(parts, flips) if flip in wanted]):
            later_tasks(where[0], range(outs[0].shape[0]), groups, q_a, q_b, used, state, store)


def attend_later(where, queries, parts, flips, running, groups):
    tokens = queries[0].shape[0]
    heads = running[0].shape[0]
    count = len(parts)
    return kernel_call(
        functools.partial(later_kernel, groups, flips),
        "attend_later",
        [f32(heads, 2 * tokens, HEAD_DIM)] * 3,
        [IN_SMEM] + [IN_VMEM] * (5 + 2 * count),
        [IN_VMEM] * 3,
        aliases={3 + 2 * count + i: i for i in range(3)},
        flops=8 * heads * tokens * sum(p[0].shape[0] for p in parts) * HEAD_DIM,
    )(where, *queries, *(ref for part in parts for ref in part), *running)


def last_kernel(heads, groups, count, flip, where, q_a, q_b, *refs):
    parts, refs = pairs(refs[: 2 * count]), refs[2 * count :]
    state_refs, outs = refs[:3], refs[3:]
    tokens = q_a.shape[0]

    def state(head):
        return tuple(ref[head] for ref in state_refs)

    def store(head, values):
        _, total, mixture = values
        result = (mixture / total).astype(jnp.bfloat16)
        place = (head - heads[0]) * HEAD_DIM
        for side, out in enumerate(outs):
            out[:, place : place + HEAD_DIM] = result[side * tokens : (side + 1) * tokens]

    @pl.when(is_earlier(where, flip))
    def _():
        later_tasks(where[0], heads, groups, q_a, q_b, parts, state, store)

    @pl.when(~is_earlier(where, flip))
    def _():
        for head in heads:
            store(head, state(head))


def attend_last(where, queries, parts, flip, running, heads, groups):
    tokens = queries[0].shape[0]
    count = len(parts)
    return kernel_call(
        functools.partial(last_kernel, heads, groups, count, flip),
        "attend_last",
        [bf16(tokens, len(heads) * HEAD_DIM)] * 2,
        [IN_SMEM] + [IN_VMEM] * (5 + 2 * count),
        [IN_VMEM] * 2,
        flops=8 * len(heads) * tokens * sum(p[0].shape[0] for p in parts) * HEAD_DIM,
    )(where, *queries, *(ref for part in parts for ref in part), *running)


def place_kernel(places, where, *refs):
    out, sem = refs[-2:]
    half = out.shape[1] // 2
    copies = []
    for part, (received, number) in zip(refs, places):
        side = 1 - where[0] if received else where[0]
        width = part.shape[1]
        columns = pl.ds(pl.multiple_of(side * half + number * width, HEAD_DIM), width)
        copies.append(pltpu.make_async_copy(part, out.at[:, columns], sem.at[len(copies)]))
    run_copies(copies)


def place_heads(where, parts, places, shape, base=None):
    begun = [] if base is None else [base]
    return kernel_call(
        functools.partial(place_kernel, places),
        "place_heads",
        bf16(*shape),
        [IN_SMEM] + [IN_VMEM] * len(parts) + [IN_PLACE] * len(begun),
        IN_PLACE,
        [pltpu.SemaphoreType.DMA((len(parts),))],
        aliases={1 + len(parts): 0} if begun else {},
    )(where, *parts, *begun)


def as_scalars(values):
    return jnp.stack([jnp.asarray(v, jnp.int32) for v in values])


def shards(seq_size, fsdp_size, clean_states, noise_mask, mask_embed, queries, w_key, w_value):
    chips = seq_size // 2
    place = lax.axis_index("seq")
    core = lax.rem(place, 2)
    chip = place // 2
    shard = lax.axis_index("fsdp")
    states = clean_states[0]
    marks = noise_mask
    tokens = states.shape[0]
    depth, kv_width = w_key.shape
    kv_heads = kv_width // 2 // HEAD_DIM

    def swap_cores(array):
        return lax.ppermute(array, "seq", [(s, s ^ 1) for s in range(seq_size)])

    def to_chip(array, flip, sources=None):
        sources = range(chips) if sources is None else sources
        pairs = [(2 * s + c, 2 * (s ^ flip) + c) for s in sources for c in range(2)]
        return lax.ppermute(array, "seq", pairs)

    def to_shard(array, flip):
        return lax.ppermute(array, "fsdp", [(s, s ^ flip) for s in range(fsdp_size)])

    square = chips == CHIPS and fsdp_size == 4
    barrier = lax.optimization_barrier
    where = as_scalars([core, chip, shard])
    query_own = queries[0]
    if square:
        quarter = depth // chips
        half = kv_width // 2
        mine = jnp.concatenate(
            [lax.dynamic_slice(w, (chip * quarter, core * half), (quarter, half)) for w in (w_key, w_value)], 1
        )
        far, near = to_shard(mine, 3), to_shard(mine, 1)

    mask_rows = jnp.broadcast_to(mask_embed[None, :], (MASK_ROWS, mask_embed.shape[0]))
    rows = (states, swap_cores(states), mask_rows)
    query_rows = (query_own, swap_cores(query_own))
    both_marks = (marks, swap_cores(marks))
    steps = jnp.arange(tokens, dtype=jnp.int32)
    cosine, sine = rotation(jnp.concatenate([place * tokens + steps, (place ^ 1) * tokens + steps]))

    if square:
        (corner,) = cut_weights(where, (3,), quarter, w_key, w_value)
        far, near, mine, corner, rows, query_rows, both_marks, cosine, sine = barrier(
            (far, near, mine, corner, rows, query_rows, both_marks, cosine, sine)
        )
        middle = to_shard(mine, 2)
        near_x, far_x = to_chip(near, 1), to_chip(far, 1)
        near_y, far_y = to_chip(near, 2), to_chip(far, 2)
        middle, corner, near_x, near_y, far_x, far_y = barrier((middle, corner, near_x, near_y, far_x, far_y))
        far_corner, near_corner = to_shard(corner, 3), to_shard(corner, 1)
        last = [to_chip(middle, flip) for flip in (3, 1, 2)]
        segments = [
            [((w_key, w_value), 0, None, depth)],
            [
                (far, 3, 0, depth),
                (far_x, 3, 1, depth),
                (far_y, 3, 2, depth),
            ],
            [(near, 1, 0, depth), (near_x, 1, 1, depth), (near_y, 1, 2, depth)],
        ]
        final = [
            [
                (far_corner, 3, 3, depth),
                (near_corner, 1, 3, depth),
                (middle, 2, 0, depth),
                (last[0], 2, 3, depth),
                (last[1], 2, 1, depth),
                (last[2], 2, 2, depth),
            ]
        ]
        staged = project_partial(rows, segments, final, where)
    else:
        (half_weights,) = cut_weights(where, (None,), depth, w_key, w_value)
        gathered = lax.all_gather(half_weights, "fsdp", axis=0, tiled=True)
        final, staged = [[(gathered, None, None, depth)]], ()
    tables = (cosine, sine)
    *clean, mask_sums = project_finish(rows, staged, final, where, tables)

    heads = query_own.shape[1] // 2 // HEAD_DIM
    groups = heads // kv_heads
    if square:
        keys, values = clean
        keys_x, keys_y = to_chip(keys, 1, (0, 1, 2)), to_chip(keys, 2, (0, 1))
        values_x, values_y = to_chip(values, 1, (0, 2)), to_chip(values, 2, (0, 1))
        running = attend_own(where, query_rows, tables, both_marks, mask_sums, clean, heads, groups)
        keys_x, running = barrier((keys_x, running))
        last_parts = [(to_chip(keys_x, 2, (0, 1)), to_chip(values_y, 1, (2, 3)))]
        along = [(keys_x, values_x), (keys_y, values_y)]
        running = attend_later(where, query_rows, along, (1, 2), running, groups)
    else:
        running = attend_own(where, query_rows, tables, both_marks, mask_sums, clean, heads, groups)
        for flip in range(1, chips):
            parts = [tuple(to_chip(part, flip, [s for s in range(chips) if s < s ^ flip]) for part in clean)]
            if flip < chips - 1:
                running = attend_later(where, query_rows, parts, (flip,), running, groups)
        last_parts = parts
    kept, received = [], []
    for first in range(0, heads, groups):
        own, other = attend_last(
            where, query_rows, last_parts, chips - 1, running, range(first, first + groups), groups
        )
        kept.append(own)
        received.append(swap_cores(other))
    parts = kept + received[:-1]
    places = [(False, i) for i in range(len(kept))] + [(True, i) for i in range(len(received) - 1)]
    output = place_heads(where, parts, places, query_own.shape)
    output = place_heads(where, received[-1:], [(True, len(received) - 1)], query_own.shape, output)
    return output[None]


def solution(mesh):
    placed = (
        P("fsdp", "seq", None),
        P("fsdp", "seq"),
        P(),
        P("fsdp", "seq", None),
        P("fsdp", None),
        P("fsdp", None),
    )
    return jax.shard_map(
        functools.partial(shards, mesh.shape["seq"], mesh.shape["fsdp"]),
        mesh=mesh,
        in_specs=placed,
        out_specs=P("fsdp", "seq", None),
        check_vma=False,
    )
```

```python
import functools
import math

import jax
import jax.numpy as jnp
from jax import lax
from jax.experimental import pallas as pl
from jax.experimental.pallas import tpu as pltpu
from jax.sharding import PartitionSpec as P

HEADS = 16
HEAD_DIM = 128
BLOCK = 256
ROPE_BASE = 500000.0
MASK_ROWS = 16
CHIPS = 4
SCORE_SCALE = HEAD_DIM**-0.5 * math.log2(math.e)
VMEM_LIMIT = 16 * 1024 * 1024
WIDE_LIMIT = 56 * 1024 * 1024

IN_VMEM = pl.BlockSpec(memory_space=pltpu.VMEM)
IN_SMEM = pl.BlockSpec(memory_space=pltpu.SMEM)
IN_PLACE = pl.BlockSpec(memory_space=pl.ANY)


def kernel_call(body, name, out_shape, in_specs, out_specs, scratch=(), aliases=None, flops=0, limit=VMEM_LIMIT):
    return pl.pallas_call(
        body,
        out_shape=out_shape,
        in_specs=in_specs,
        out_specs=out_specs,
        scratch_shapes=scratch,
        input_output_aliases=aliases or {},
        compiler_params=pltpu.CompilerParams(vmem_limit_bytes=limit),
        cost_estimate=pl.CostEstimate(flops=flops, bytes_accessed=0, transcendentals=0),
        name=name,
    )


def bf16(*shape):
    return jax.ShapeDtypeStruct(shape, jnp.bfloat16)


def f32(*shape):
    return jax.ShapeDtypeStruct(shape, jnp.float32)


def rotation(positions):
    half_dim = HEAD_DIM // 2
    frequency = ROPE_BASE ** (-(jnp.arange(half_dim, dtype=jnp.float32) * 2.0 / HEAD_DIM))
    angles = positions.astype(jnp.float32)[:, None] * frequency[None, :]
    cosine = jnp.cos(angles)
    sine = jnp.sin(angles)
    return jnp.concatenate([cosine, cosine], -1), jnp.concatenate([-sine, sine], -1)


def run_copies(copies):
    for copy in copies:
        copy.start()
    for copy in copies:
        copy.wait()


def core_columns(where, weight):
    half = weight.shape[1] // 2
    return pl.ds(pl.multiple_of(where[0] * half, HEAD_DIM), half)


def cut_kernel(flips, where, key_ref, value_ref, *refs):
    outs, sem = refs[:-1], refs[-1]
    columns = core_columns(where, key_ref)
    copies = []
    for out, flip in zip(outs, flips):
        size, width = out.shape
        first = 0 if flip is None else pl.multiple_of((where[1] ^ flip) * size, 16)
        for side, weight in enumerate((key_ref, value_ref)):
            target = out.at[:, side * (width // 2) : (side + 1) * (width // 2)]
            copies.append(pltpu.make_async_copy(weight.at[pl.ds(first, size), columns], target, sem.at[len(copies)]))
    run_copies(copies)


def cut_weights(where, flips, size, w_key, w_value):
    return kernel_call(
        functools.partial(cut_kernel, flips),
        "cut_weights",
        [bf16(size, w_key.shape[1])] * len(flips),
        [IN_SMEM, IN_PLACE, IN_PLACE],
        [IN_VMEM] * len(flips),
        [pltpu.SemaphoreType.DMA((2 * len(flips),))],
        limit=WIDE_LIMIT,
    )(where, w_key, w_value)


def fetch(segments, where, rows, refs, rows_held, held, sem):
    refs = list(refs)
    place = number = 0
    waits = []
    for pieces in segments:
        copies = []
        start_at = place
        for shard_flip, chip_flip, depth, size, as_given in pieces:
            first = 0 if shard_flip is None else (where[2] ^ shard_flip) * depth
            if chip_flip is not None:
                first = first + (where[1] ^ chip_flip) * size
            columns = pl.ds(first if isinstance(first, int) else pl.multiple_of(first, HEAD_DIM), size)
            into = slice(place, place + size)
            low = 0
            for part in rows:
                copies.append((part.at[:, columns], rows_held.at[low : low + part.shape[0], into]))
                low += part.shape[0]
            if held is None:
                pass
            elif as_given:
                for side in range(2):
                    weight = refs.pop(0)
                    half = weight.shape[1] // 2
                    target = held.at[into, side * half : (side + 1) * half]
                    copies.append((weight.at[:, core_columns(where, weight)], target))
            else:
                copies.append((refs.pop(0), held.at[into, :]))
            place += size
        copies = [pltpu.make_async_copy(a, b, sem.at[number + i]) for i, (a, b) in enumerate(copies)]
        number += len(copies)
        for copy in copies:
            copy.start()
        waits.append((copies, slice(start_at, place)))
    return waits


def products(waits, rows_held, held, total):
    for copies, into in waits:
        for copy in copies:
            copy.wait()
        term = jnp.dot(rows_held[:, into], held[into, :], preferred_element_type=jnp.float32)
        total = term if total is None else total + term
    return total


def partial_kernel(segments, final, count, where, states, other, masks, *refs):
    total_ref, final_rows, rows_held, held, sem, final_sem = refs[count:]
    rows = (states, other, masks)
    waits = fetch(segments, where, rows, refs[:count], rows_held, held, sem)
    final_waits = fetch(final, where, rows, (), final_rows, None, final_sem)
    total_ref[...] = products(waits, rows_held, held, None)
    for copies, _ in final_waits:
        for copy in copies:
            copy.wait()


def rotated(key, cosine, sine):
    return key * cosine + pltpu.roll(key, HEAD_DIM // 2, 1) * sine


def finish_kernel(segments, count, staged, tokens, where, *refs):
    if staged:
        total_ref, rows_held = refs[:2]
        rows, total, refs = (), total_ref[...], refs[2:]
    else:
        rows, total, refs = refs[:3], None, refs[3:]
    pieces, (cos_ref, sin_ref, *refs) = refs[:count], refs[count:]
    clean_out, mask_out, refs = refs[0], refs[1], refs[2:]
    if not staged:
        rows_held, *refs = refs
    held, kept, sem, out_sem = refs
    waits = fetch(segments, where, rows, pieces, rows_held, held, sem)
    sums = products(waits, rows_held, held, total)
    kv_heads = sums.shape[1] // 2 // HEAD_DIM
    writes = []
    for side in range(2):
        mine = slice(side * tokens, (side + 1) * tokens)
        for head in range(kv_heads):
            for is_value in range(2):
                first = (is_value * kv_heads + head) * HEAD_DIM
                part = sums[mine, first : first + HEAD_DIM]
                if not is_value:
                    part = rotated(part, cos_ref[mine, :], sin_ref[mine, :])
                place = (2 * head + is_value) * HEAD_DIM
                kept[side, :, place : place + HEAD_DIM] = part.astype(jnp.bfloat16)
        writes.append(pltpu.make_async_copy(kept.at[side], clean_out.at[mine, :], out_sem.at[side]))
        writes[-1].start()
    mask_out[...] = sums[2 * tokens : 2 * tokens + 8]
    for write in writes:
        write.wait()


def describe(segments):
    kinds, arrays, copies = [], [], 0
    for segment in segments:
        kinds.append([])
        for piece, shard_flip, chip_flip, depth in segment:
            as_given = isinstance(piece, tuple)
            arrays.extend(piece if as_given else (piece,))
            kinds[-1].append((shard_flip, chip_flip, depth, arrays[-1].shape[0], as_given))
            copies += 5 if as_given else 4
    return kinds, arrays, sum(kind[3] for segment in kinds for kind in segment), copies


def project_partial(rows, segments, final, where):
    kinds, arrays, inner, copies = describe(segments)
    final_kinds, _, final_inner, final_copies = describe(final)
    width = arrays[0].shape[1]
    height = sum(r.shape[0] for r in rows)
    return kernel_call(
        functools.partial(partial_kernel, kinds, final_kinds, len(arrays)),
        "project_partial",
        [f32(height, width), bf16(height, final_inner)],
        [IN_SMEM] + [IN_PLACE] * (3 + len(arrays)),
        [IN_VMEM] * 2,
        [
            pltpu.VMEM((height, inner), jnp.bfloat16),
            pltpu.VMEM((inner, width), jnp.bfloat16),
            pltpu.SemaphoreType.DMA((copies,)),
            pltpu.SemaphoreType.DMA((final_copies,)),
        ],
        flops=2 * width * inner * height,
    )(where, *rows, *arrays)


def project_finish(rows, staged, segments, where, ending):
    kinds, arrays, inner, copies = describe(segments)
    width = arrays[0].shape[1]
    tokens = rows[0].shape[0]
    height = sum(r.shape[0] for r in rows)
    scratch = [] if staged else [pltpu.VMEM((height, inner), jnp.bfloat16)]
    begin = staged or rows
    return kernel_call(
        functools.partial(finish_kernel, kinds, len(arrays), bool(staged), tokens),
        "project_finish",
        [bf16(2 * tokens, width), f32(8, width)],
        [IN_SMEM] + [IN_VMEM if staged else IN_PLACE] * len(begin) + [IN_PLACE] * len(arrays) + [IN_VMEM] * len(ending),
        [IN_PLACE, IN_VMEM],
        [
            *scratch,
            pltpu.VMEM((inner, width), jnp.bfloat16),
            pltpu.VMEM((2, tokens, width), jnp.bfloat16),
            pltpu.SemaphoreType.DMA((copies,)),
            pltpu.SemaphoreType.DMA((2,)),
        ],
        flops=2 * width * inner * height,
    )(where, *begin, *arrays, *ending)


def scores_of(query, key):
    return lax.dot_general(query, key, (((1,), (1,)), ((), ())), preferred_element_type=jnp.float32)


def lane_tiles(array):
    return [array[:, lane : lane + HEAD_DIM] for lane in range(0, array.shape[1], HEAD_DIM)]


def absorb(scores, values, before):
    tiles = [lane_tiles(s) for s in scores]
    peak = functools.reduce(jnp.maximum, [t for part in tiles for t in part])
    top = jnp.broadcast_to(jnp.max(peak, -1, keepdims=True), peak.shape) * SCORE_SCALE
    if before is not None:
        top = jnp.maximum(top, before[0])
    both = None
    for part, value in zip(tiles, values):
        weights = jnp.concatenate([jnp.exp2(t * SCORE_SCALE - top).astype(jnp.bfloat16) for t in part], 1)
        wide = jnp.concatenate([value, jnp.ones_like(value)], 1)
        term = jnp.dot(weights, wide, preferred_element_type=jnp.float32)
        both = term if both is None else both + term
    mixture, total = both[:, :HEAD_DIM], both[:, HEAD_DIM:]
    if before is not None:
        rescale = jnp.exp2(before[0] - top)
        total = before[1] * rescale + total
        mixture = before[2] * rescale + mixture
    return top, total, mixture


def pipelined(tasks, score, use):
    waiting = None
    for task in tasks:
        scores = score(task)
        if waiting is not None:
            use(*waiting)
        waiting = (task, scores)
    use(*waiting)


def query_of(query_ref, core, head):
    first = core * (query_ref.shape[1] // 2) + head * HEAD_DIM
    return query_ref[:, pl.ds(pl.multiple_of(first, HEAD_DIM), HEAD_DIM)]


def kv_lanes(groups, head, is_value):
    first = (2 * (head // groups) + is_value) * HEAD_DIM
    return slice(first, first + HEAD_DIM)


def own_kernel(groups, where, q_a, q_b, cos_ref, sin_ref, marks_a, marks_b, mask_ref, *refs):
    clean_in, state, (clean_ref, noisy_ref, sem) = refs[0], refs[1:4], refs[4:]
    core = where[0]
    tokens = q_a.shape[0]
    heads = state[0].shape[0]
    run_copies(
        [
            pltpu.make_async_copy(clean_in.at[i * tokens : (i + 1) * tokens, :], clean_ref.at[i], sem.at[i])
            for i in range(2)
        ]
    )
    for side, marks in enumerate((marks_a, marks_b)):
        mine = slice(side * tokens, (side + 1) * tokens)
        masked = jnp.broadcast_to(marks[...].astype(jnp.float32), (HEAD_DIM, tokens)).T > 0.5
        for head in range(heads // groups):
            for is_value in range(2):
                first = (is_value * (heads // groups) + head) * HEAD_DIM
                token = jnp.broadcast_to(mask_ref[:1, first : first + HEAD_DIM], (tokens, HEAD_DIM))
                if not is_value:
                    token = rotated(token, cos_ref[mine, :], sin_ref[mine, :])
                lanes = kv_lanes(groups, head * groups, is_value)
                clean = clean_ref[side, :, lanes].astype(jnp.float32)
                noisy_ref[side, :, lanes] = jnp.where(masked, token, clean).astype(jnp.bfloat16)

    def score(task):
        head, side = task
        query = query_of((q_a, q_b)[side], core, head)
        lanes = kv_lanes(groups, head, 0)
        near = scores_of(query, noisy_ref[side, :, lanes])
        far = scores_of(query, clean_ref[1 - side, :, lanes])
        return [near, jnp.where(core == 1 - side, far, -1e30)]

    def use(task, scores):
        head, side = task
        lanes = kv_lanes(groups, head, 1)
        values = [noisy_ref[side, :, lanes], clean_ref[1 - side, :, lanes]]
        mine = pl.ds(side * tokens, tokens)
        for ref, value in zip(state, absorb(scores, values, None)):
            ref[head, mine, :] = value

    pipelined([(head, side) for head in range(heads) for side in range(2)], score, use)


def attend_own(where, queries, tables, marks, mask_sums, clean, heads, groups):
    tokens = queries[0].shape[0]
    return kernel_call(
        functools.partial(own_kernel, groups),
        "attend_own",
        [f32(heads, 2 * tokens, HEAD_DIM)] * 3,
        [IN_SMEM] + [IN_VMEM] * 7 + [IN_PLACE],
        [IN_VMEM] * 3,
        [pltpu.VMEM((2, tokens, clean.shape[1]), jnp.bfloat16)] * 2 + [pltpu.SemaphoreType.DMA((2,))],
        flops=16 * heads * tokens * tokens * HEAD_DIM,
    )(where, *queries, *tables, *marks, mask_sums, clean)


def later_tasks(core, heads, groups, q_a, q_b, parts, state, store):
    def score(head):
        query = jnp.concatenate([query_of(q, core, head) for q in (q_a, q_b)], 0)
        return [scores_of(query, part[:, kv_lanes(groups, head, 0)]) for part in parts]

    def use(head, scores):
        store(head, absorb(scores, [part[:, kv_lanes(groups, head, 1)] for part in parts], state(head)))

    pipelined(heads, score, use)


def is_earlier(where, flip):
    return (where[1] ^ flip) < where[1]


def later_kernel(groups, flips, where, q_a, q_b, *refs):
    count = len(flips)
    parts, outs = refs[:count], refs[count + 3 :]

    def state(head):
        return tuple(out[head] for out in outs)

    def store(head, values):
        for out, value in zip(outs, values):
            out[head] = value

    chips = sorted(set(flips))
    for chosen in range(1, 1 << len(chips)):
        wanted = [flip for number, flip in enumerate(chips) if chosen >> number & 1]
        hits = [is_earlier(where, flip) if flip in wanted else ~is_earlier(where, flip) for flip in chips]

        @pl.when(functools.reduce(jnp.logical_and, hits))
        def _(used=[part for part, flip in zip(parts, flips) if flip in wanted]):
            later_tasks(where[0], range(outs[0].shape[0]), groups, q_a, q_b, used, state, store)


def attend_later(where, queries, parts, flips, running, groups):
    tokens = queries[0].shape[0]
    heads = running[0].shape[0]
    count = len(parts)
    return kernel_call(
        functools.partial(later_kernel, groups, flips),
        "attend_later",
        [f32(heads, 2 * tokens, HEAD_DIM)] * 3,
        [IN_SMEM] + [IN_VMEM] * (5 + count),
        [IN_VMEM] * 3,
        aliases={3 + count + i: i for i in range(3)},
        flops=8 * heads * tokens * sum(p.shape[0] for p in parts) * HEAD_DIM,
    )(where, *queries, *parts, *running)


def last_kernel(heads, groups, count, flip, where, q_a, q_b, *refs):
    parts, state_refs, outs = refs[:count], refs[count : count + 3], refs[count + 3 :]
    tokens = q_a.shape[0]

    def state(head):
        return tuple(ref[head] for ref in state_refs)

    def store(head, values):
        _, total, mixture = values
        result = (mixture / total).astype(jnp.bfloat16)
        place = (head - heads[0]) * HEAD_DIM
        for side, out in enumerate(outs):
            out[:, place : place + HEAD_DIM] = result[side * tokens : (side + 1) * tokens]

    @pl.when(is_earlier(where, flip))
    def _():
        later_tasks(where[0], heads, groups, q_a, q_b, parts, state, store)

    @pl.when(~is_earlier(where, flip))
    def _():
        for head in heads:
            store(head, state(head))


def attend_last(where, queries, parts, flip, running, heads, groups):
    tokens = queries[0].shape[0]
    count = len(parts)
    return kernel_call(
        functools.partial(last_kernel, heads, groups, count, flip),
        "attend_last",
        [bf16(tokens, len(heads) * HEAD_DIM)] * 2,
        [IN_SMEM] + [IN_VMEM] * (5 + count),
        [IN_VMEM] * 2,
        flops=8 * len(heads) * tokens * sum(p.shape[0] for p in parts) * HEAD_DIM,
    )(where, *queries, *parts, *running)


def place_kernel(places, where, *refs):
    out, sem = refs[-2:]
    half = out.shape[1] // 2
    copies = []
    for part, (received, number) in zip(refs, places):
        side = 1 - where[0] if received else where[0]
        width = part.shape[1]
        columns = pl.ds(pl.multiple_of(side * half + number * width, HEAD_DIM), width)
        copies.append(pltpu.make_async_copy(part, out.at[:, columns], sem.at[len(copies)]))
    run_copies(copies)


def place_heads(where, parts, places, shape, base=None):
    begun = [] if base is None else [base]
    return kernel_call(
        functools.partial(place_kernel, places),
        "place_heads",
        bf16(*shape),
        [IN_SMEM] + [IN_VMEM] * len(parts) + [IN_PLACE] * len(begun),
        IN_PLACE,
        [pltpu.SemaphoreType.DMA((len(parts),))],
        aliases={1 + len(parts): 0} if begun else {},
    )(where, *parts, *begun)


def as_scalars(values):
    return jnp.stack([jnp.asarray(v, jnp.int32) for v in values])


def shards(seq_size, fsdp_size, clean_states, noise_mask, mask_embed, queries, w_key, w_value):
    chips = seq_size // 2
    place = lax.axis_index("seq")
    core = lax.rem(place, 2)
    chip = place // 2
    shard = lax.axis_index("fsdp")
    states = clean_states[0]
    marks = noise_mask
    tokens = states.shape[0]
    depth, kv_width = w_key.shape
    kv_heads = kv_width // 2 // HEAD_DIM

    def swap_cores(array):
        return lax.ppermute(array, "seq", [(s, s ^ 1) for s in range(seq_size)])

    def to_chip(array, flip, sources=None):
        sources = range(chips) if sources is None else sources
        pairs = [(2 * s + c, 2 * (s ^ flip) + c) for s in sources for c in range(2)]
        return lax.ppermute(array, "seq", pairs)

    def to_shard(array, flip):
        return lax.ppermute(array, "fsdp", [(s, s ^ flip) for s in range(fsdp_size)])

    square = chips == CHIPS and fsdp_size == 4
    barrier = lax.optimization_barrier
    where = as_scalars([core, chip, shard])
    query_own = queries[0]
    if square:
        quarter = depth // chips
        half = kv_width // 2
        mine = jnp.concatenate(
            [lax.dynamic_slice(w, (chip * quarter, core * half), (quarter, half)) for w in (w_key, w_value)], 1
        )
        far, near = to_shard(mine, 3), to_shard(mine, 1)

    mask_rows = jnp.broadcast_to(mask_embed[None, :], (MASK_ROWS, mask_embed.shape[0]))
    rows = (states, swap_cores(states), mask_rows)
    query_rows = (query_own, swap_cores(query_own))
    both_marks = (marks, swap_cores(marks))
    steps = jnp.arange(tokens, dtype=jnp.int32)
    cosine, sine = rotation(jnp.concatenate([place * tokens + steps, (place ^ 1) * tokens + steps]))

    if square:
        (corner,) = cut_weights(where, (3,), quarter, w_key, w_value)
        far, near, mine, corner, rows, query_rows, both_marks, cosine, sine = barrier(
            (far, near, mine, corner, rows, query_rows, both_marks, cosine, sine)
        )
        middle = to_shard(mine, 2)
        near_x, far_x = to_chip(near, 1), to_chip(far, 1)
        near_y, far_y = to_chip(near, 2), to_chip(far, 2)
        middle, corner, near_x, near_y, far_x, far_y = barrier((middle, corner, near_x, near_y, far_x, far_y))
        far_corner, near_corner = to_shard(corner, 3), to_shard(corner, 1)
        last = [to_chip(middle, flip) for flip in (3, 1, 2)]
        segments = [
            [((w_key, w_value), 0, None, depth)],
            [
                (far, 3, 0, depth),
                (far_x, 3, 1, depth),
                (far_y, 3, 2, depth),
            ],
            [(near, 1, 0, depth), (near_x, 1, 1, depth), (near_y, 1, 2, depth)],
        ]
        final = [
            [
                (middle, 2, 0, depth),
                (last[0], 2, 3, depth),
                (last[1], 2, 1, depth),
                (last[2], 2, 2, depth),
                (near_corner, 1, 3, depth),
                (far_corner, 3, 3, depth),
            ]
        ]
        staged = project_partial(rows, segments, final, where)
    else:
        (half_weights,) = cut_weights(where, (None,), depth, w_key, w_value)
        gathered = lax.all_gather(half_weights, "fsdp", axis=0, tiled=True)
        final, staged = [[(gathered, None, None, depth)]], ()
    tables = (cosine, sine)
    clean, mask_sums = project_finish(rows, staged, final, where, tables)

    heads = query_own.shape[1] // 2 // HEAD_DIM
    groups = heads // kv_heads
    if square:
        along_x, along_y = to_chip(clean, 1, (0, 1, 2)), to_chip(clean, 2, (0, 1))
        running = attend_own(where, query_rows, tables, both_marks, mask_sums, clean, heads, groups)
        along_x, along_y, running = barrier((along_x, along_y, running))
        last_parts = [to_chip(along_x[:tokens], 2, (0, 1)), to_chip(along_y[tokens:], 1, (2, 3))]
        running = attend_later(where, query_rows, [along_x, along_y], (1, 2), running, groups)
    else:
        running = attend_own(where, query_rows, tables, both_marks, mask_sums, clean, heads, groups)
        for flip in range(1, chips):
            parts = [to_chip(clean, flip, [s for s in range(chips) if s < s ^ flip])]
            if flip < chips - 1:
                running = attend_later(where, query_rows, parts, (flip,), running, groups)
        last_parts = parts
    kept, received = [], []
    for first in range(0, heads, groups):
        own, other = attend_last(
            where, query_rows, last_parts, chips - 1, running, range(first, first + groups), groups
        )
        kept.append(own)
        received.append(swap_cores(other))
    parts = kept + received[:-1]
    places = [(False, i) for i in range(len(kept))] + [(True, i) for i in range(len(received) - 1)]
    output = place_heads(where, parts, places, query_own.shape)
    output = place_heads(where, received[-1:], [(True, len(received) - 1)], query_own.shape, output)
    return output[None]


def solution(mesh):
    placed = (
        P("fsdp", "seq", None),
        P("fsdp", "seq"),
        P(),
        P("fsdp", "seq", None),
        P("fsdp", None),
        P("fsdp", None),
    )
    return jax.shard_map(
        functools.partial(shards, mesh.shape["seq"], mesh.shape["fsdp"]),
        mesh=mesh,
        in_specs=placed,
        out_specs=P("fsdp", "seq", None),
        check_vma=False,
    )
```

```python
import functools
import math

import jax
import jax.numpy as jnp
from jax import lax
from jax.experimental import pallas as pl
from jax.experimental.pallas import tpu as pltpu
from jax.sharding import PartitionSpec as P

HEADS = 16
HEAD_DIM = 128
BLOCK = 256
ROPE_BASE = 500000.0
MASK_ROWS = 16
CHIPS = 4
SCORE_SCALE = HEAD_DIM**-0.5 * math.log2(math.e)
VMEM_LIMIT = 16 * 1024 * 1024
WIDE_LIMIT = 56 * 1024 * 1024

IN_VMEM = pl.BlockSpec(memory_space=pltpu.VMEM)
IN_SMEM = pl.BlockSpec(memory_space=pltpu.SMEM)
IN_PLACE = pl.BlockSpec(memory_space=pl.ANY)


def kernel_call(body, name, out_shape, in_specs, out_specs, scratch=(), aliases=None, flops=0, limit=VMEM_LIMIT):
    return pl.pallas_call(
        body,
        out_shape=out_shape,
        in_specs=in_specs,
        out_specs=out_specs,
        scratch_shapes=scratch,
        input_output_aliases=aliases or {},
        compiler_params=pltpu.CompilerParams(vmem_limit_bytes=limit),
        cost_estimate=pl.CostEstimate(flops=flops, bytes_accessed=0, transcendentals=0),
        name=name,
    )


def bf16(*shape):
    return jax.ShapeDtypeStruct(shape, jnp.bfloat16)


def f32(*shape):
    return jax.ShapeDtypeStruct(shape, jnp.float32)


def rotation(positions):
    half_dim = HEAD_DIM // 2
    frequency = ROPE_BASE ** (-(jnp.arange(half_dim, dtype=jnp.float32) * 2.0 / HEAD_DIM))
    angles = positions.astype(jnp.float32)[:, None] * frequency[None, :]
    cosine = jnp.cos(angles)
    sine = jnp.sin(angles)
    return jnp.concatenate([cosine, cosine], -1), jnp.concatenate([-sine, sine], -1)


def run_copies(copies):
    for copy in copies:
        copy.start()
    for copy in copies:
        copy.wait()


def core_columns(where, weight):
    half = weight.shape[1] // 2
    return pl.ds(pl.multiple_of(where[0] * half, HEAD_DIM), half)


def cut_kernel(flips, where, key_ref, value_ref, *refs):
    outs, sem = refs[:-1], refs[-1]
    columns = core_columns(where, key_ref)
    copies = []
    for out, flip in zip(outs, flips):
        size, width = out.shape
        first = 0 if flip is None else pl.multiple_of((where[1] ^ flip) * size, 16)
        for side, weight in enumerate((key_ref, value_ref)):
            target = out.at[:, side * (width // 2) : (side + 1) * (width // 2)]
            copies.append(pltpu.make_async_copy(weight.at[pl.ds(first, size), columns], target, sem.at[len(copies)]))
    run_copies(copies)


def cut_weights(where, flips, size, w_key, w_value):
    return kernel_call(
        functools.partial(cut_kernel, flips),
        "cut_weights",
        [bf16(size, w_key.shape[1])] * len(flips),
        [IN_SMEM, IN_PLACE, IN_PLACE],
        [IN_VMEM] * len(flips),
        [pltpu.SemaphoreType.DMA((2 * len(flips),))],
        limit=WIDE_LIMIT,
    )(where, w_key, w_value)


def fetch(segments, where, rows, refs, rows_held, held, sem):
    refs = list(refs)
    place = number = 0
    waits = []
    for pieces in segments:
        copies = []
        start_at = place
        for shard_flip, chip_flip, depth, size, as_given in pieces:
            first = 0 if shard_flip is None else (where[2] ^ shard_flip) * depth
            if chip_flip is not None:
                first = first + (where[1] ^ chip_flip) * size
            columns = pl.ds(first if isinstance(first, int) else pl.multiple_of(first, HEAD_DIM), size)
            into = slice(place, place + size)
            low = 0
            for part in rows:
                copies.append((part.at[:, columns], rows_held.at[low : low + part.shape[0], into]))
                low += part.shape[0]
            if held is None:
                pass
            elif as_given:
                for side in range(2):
                    weight = refs.pop(0)
                    half = weight.shape[1] // 2
                    target = held.at[into, side * half : (side + 1) * half]
                    copies.append((weight.at[:, core_columns(where, weight)], target))
            else:
                copies.append((refs.pop(0), held.at[into, :]))
            place += size
        copies = [pltpu.make_async_copy(a, b, sem.at[number + i]) for i, (a, b) in enumerate(copies)]
        number += len(copies)
        for copy in copies:
            copy.start()
        waits.append((copies, slice(start_at, place)))
    return waits


def products(waits, rows_held, held, total):
    for copies, into in waits:
        for copy in copies:
            copy.wait()
        term = jnp.dot(rows_held[:, into], held[into, :], preferred_element_type=jnp.float32)
        total = term if total is None else total + term
    return total


def partial_kernel(segments, final, count, where, states, other, masks, *refs):
    total_ref, final_rows, rows_held, held, sem, final_sem = refs[count:]
    rows = (states, other, masks)
    waits = fetch(segments, where, rows, refs[:count], rows_held, held, sem)
    final_waits = fetch(final, where, rows, (), final_rows, None, final_sem)
    total_ref[...] = products(waits, rows_held, held, None)
    for copies, _ in final_waits:
        for copy in copies:
            copy.wait()


def rotated(key, cosine, sine):
    return key * cosine + pltpu.roll(key, HEAD_DIM // 2, 1) * sine


def finish_kernel(segments, count, staged, tokens, where, *refs):
    if staged:
        total_ref, rows_held = refs[:2]
        rows, total, refs = (), total_ref[...], refs[2:]
    else:
        rows, total, refs = refs[:3], None, refs[3:]
    pieces, (cos_ref, sin_ref, *refs) = refs[:count], refs[count:]
    clean_out, mask_out, refs = refs[0], refs[1], refs[2:]
    if not staged:
        rows_held, *refs = refs
    held, kept, sem, out_sem = refs
    waits = fetch(segments, where, rows, pieces, rows_held, held, sem)
    sums = products(waits, rows_held, held, total)
    kv_heads = sums.shape[1] // 2 // HEAD_DIM
    writes = []
    for side in range(2):
        mine = slice(side * tokens, (side + 1) * tokens)
        for head in range(kv_heads):
            for is_value in range(2):
                first = (is_value * kv_heads + head) * HEAD_DIM
                part = sums[mine, first : first + HEAD_DIM]
                if not is_value:
                    part = rotated(part, cos_ref[mine, :], sin_ref[mine, :])
                place = (2 * head + is_value) * HEAD_DIM
                kept[side, :, place : place + HEAD_DIM] = part.astype(jnp.bfloat16)
        writes.append(pltpu.make_async_copy(kept.at[side], clean_out.at[mine, :], out_sem.at[side]))
        writes[-1].start()
    mask_out[...] = sums[2 * tokens : 2 * tokens + 8]
    for write in writes:
        write.wait()


def describe(segments):
    kinds, arrays, copies = [], [], 0
    for segment in segments:
        kinds.append([])
        for piece, shard_flip, chip_flip, depth in segment:
            as_given = isinstance(piece, tuple)
            arrays.extend(piece if as_given else (piece,))
            kinds[-1].append((shard_flip, chip_flip, depth, arrays[-1].shape[0], as_given))
            copies += 5 if as_given else 4
    return kinds, arrays, sum(kind[3] for segment in kinds for kind in segment), copies


def project_partial(rows, segments, final, where):
    kinds, arrays, inner, copies = describe(segments)
    final_kinds, _, final_inner, final_copies = describe(final)
    width = arrays[0].shape[1]
    height = sum(r.shape[0] for r in rows)
    return kernel_call(
        functools.partial(partial_kernel, kinds, final_kinds, len(arrays)),
        "project_partial",
        [f32(height, width), bf16(height, final_inner)],
        [IN_SMEM] + [IN_PLACE] * (3 + len(arrays)),
        [IN_VMEM] * 2,
        [
            pltpu.VMEM((height, inner), jnp.bfloat16),
            pltpu.VMEM((inner, width), jnp.bfloat16),
            pltpu.SemaphoreType.DMA((copies,)),
            pltpu.SemaphoreType.DMA((final_copies,)),
        ],
        flops=2 * width * inner * height,
    )(where, *rows, *arrays)


def project_finish(rows, staged, segments, where, ending):
    kinds, arrays, inner, copies = describe(segments)
    width = arrays[0].shape[1]
    tokens = rows[0].shape[0]
    height = sum(r.shape[0] for r in rows)
    scratch = [] if staged else [pltpu.VMEM((height, inner), jnp.bfloat16)]
    begin = staged or rows
    return kernel_call(
        functools.partial(finish_kernel, kinds, len(arrays), bool(staged), tokens),
        "project_finish",
        [bf16(2 * tokens, width), f32(8, width)],
        [IN_SMEM] + [IN_VMEM if staged else IN_PLACE] * len(begin) + [IN_PLACE] * len(arrays) + [IN_VMEM] * len(ending),
        [IN_PLACE, IN_VMEM],
        [
            *scratch,
            pltpu.VMEM((inner, width), jnp.bfloat16),
            pltpu.VMEM((2, tokens, width), jnp.bfloat16),
            pltpu.SemaphoreType.DMA((copies,)),
            pltpu.SemaphoreType.DMA((2,)),
        ],
        flops=2 * width * inner * height,
    )(where, *begin, *arrays, *ending)


def scores_of(query, key):
    return lax.dot_general(query, key, (((1,), (1,)), ((), ())), preferred_element_type=jnp.float32)


def lane_tiles(array):
    return [array[:, lane : lane + HEAD_DIM] for lane in range(0, array.shape[1], HEAD_DIM)]


def absorb(scores, values, before):
    tiles = [lane_tiles(s) for s in scores]
    peak = functools.reduce(jnp.maximum, [t for part in tiles for t in part])
    top = jnp.broadcast_to(jnp.max(peak, -1, keepdims=True), peak.shape) * SCORE_SCALE
    if before is not None:
        top = jnp.maximum(top, before[0])
    both = None
    for part, value in zip(tiles, values):
        weights = jnp.concatenate([jnp.exp2(t * SCORE_SCALE - top).astype(jnp.bfloat16) for t in part], 1)
        wide = jnp.concatenate([value, jnp.ones_like(value)], 1)
        term = jnp.dot(weights, wide, preferred_element_type=jnp.float32)
        both = term if both is None else both + term
    mixture, total = both[:, :HEAD_DIM], both[:, HEAD_DIM:]
    if before is not None:
        rescale = jnp.exp2(before[0] - top)
        total = before[1] * rescale + total
        mixture = before[2] * rescale + mixture
    return top, total, mixture


def pipelined(tasks, score, use):
    waiting = None
    for task in tasks:
        scores = score(task)
        if waiting is not None:
            use(*waiting)
        waiting = (task, scores)
    use(*waiting)


def query_of(query_ref, core, head):
    first = core * (query_ref.shape[1] // 2) + head * HEAD_DIM
    return query_ref[:, pl.ds(pl.multiple_of(first, HEAD_DIM), HEAD_DIM)]


def kv_lanes(groups, head, is_value):
    first = (2 * (head // groups) + is_value) * HEAD_DIM
    return slice(first, first + HEAD_DIM)


def own_kernel(groups, where, q_a, q_b, cos_ref, sin_ref, marks_a, marks_b, mask_ref, *refs):
    clean_in, state, (clean_ref, noisy_ref, sem) = refs[0], refs[1:4], refs[4:]
    core = where[0]
    tokens = q_a.shape[0]
    heads = state[0].shape[0]
    run_copies(
        [
            pltpu.make_async_copy(clean_in.at[i * tokens : (i + 1) * tokens, :], clean_ref.at[i], sem.at[i])
            for i in range(2)
        ]
    )
    for side, marks in enumerate((marks_a, marks_b)):
        mine = slice(side * tokens, (side + 1) * tokens)
        masked = jnp.broadcast_to(marks[...].astype(jnp.float32), (HEAD_DIM, tokens)).T > 0.5
        for head in range(heads // groups):
            for is_value in range(2):
                first = (is_value * (heads // groups) + head) * HEAD_DIM
                token = jnp.broadcast_to(mask_ref[:1, first : first + HEAD_DIM], (tokens, HEAD_DIM))
                if not is_value:
                    token = rotated(token, cos_ref[mine, :], sin_ref[mine, :])
                lanes = kv_lanes(groups, head * groups, is_value)
                clean = clean_ref[side, :, lanes].astype(jnp.float32)
                noisy_ref[side, :, lanes] = jnp.where(masked, token, clean).astype(jnp.bfloat16)

    def score(task):
        head, side = task
        query = query_of((q_a, q_b)[side], core, head)
        lanes = kv_lanes(groups, head, 0)
        near = scores_of(query, noisy_ref[side, :, lanes])
        far = scores_of(query, clean_ref[1 - side, :, lanes])
        return [near, jnp.where(core == 1 - side, far, -1e30)]

    def use(task, scores):
        head, side = task
        lanes = kv_lanes(groups, head, 1)
        values = [noisy_ref[side, :, lanes], clean_ref[1 - side, :, lanes]]
        mine = pl.ds(side * tokens, tokens)
        for ref, value in zip(state, absorb(scores, values, None)):
            ref[head, mine, :] = value

    pipelined([(head, side) for head in range(heads) for side in range(2)], score, use)


def attend_own(where, queries, tables, marks, mask_sums, clean, heads, groups):
    tokens = queries[0].shape[0]
    return kernel_call(
        functools.partial(own_kernel, groups),
        "attend_own",
        [f32(heads, 2 * tokens, HEAD_DIM)] * 3,
        [IN_SMEM] + [IN_VMEM] * 7 + [IN_PLACE],
        [IN_VMEM] * 3,
        [pltpu.VMEM((2, tokens, clean.shape[1]), jnp.bfloat16)] * 2 + [pltpu.SemaphoreType.DMA((2,))],
        flops=16 * heads * tokens * tokens * HEAD_DIM,
    )(where, *queries, *tables, *marks, mask_sums, clean)


def later_tasks(core, heads, groups, q_a, q_b, parts, state, store):
    def score(head):
        query = jnp.concatenate([query_of(q, core, head) for q in (q_a, q_b)], 0)
        return [scores_of(query, part[:, kv_lanes(groups, head, 0)]) for part in parts]

    def use(head, scores):
        store(head, absorb(scores, [part[:, kv_lanes(groups, head, 1)] for part in parts], state(head)))

    pipelined(heads, score, use)


def is_earlier(where, flip):
    return (where[1] ^ flip) < where[1]


def later_kernel(groups, flips, where, q_a, q_b, *refs):
    count = len(flips)
    parts, outs = refs[:count], refs[count + 3 :]

    def state(head):
        return tuple(out[head] for out in outs)

    def store(head, values):
        for out, value in zip(outs, values):
            out[head] = value

    chips = sorted(set(flips))
    for chosen in range(1, 1 << len(chips)):
        wanted = [flip for number, flip in enumerate(chips) if chosen >> number & 1]
        hits = [is_earlier(where, flip) if flip in wanted else ~is_earlier(where, flip) for flip in chips]

        @pl.when(functools.reduce(jnp.logical_and, hits))
        def _(used=[part for part, flip in zip(parts, flips) if flip in wanted]):
            later_tasks(where[0], range(outs[0].shape[0]), groups, q_a, q_b, used, state, store)


def attend_later(where, queries, parts, flips, running, groups):
    tokens = queries[0].shape[0]
    heads = running[0].shape[0]
    count = len(parts)
    return kernel_call(
        functools.partial(later_kernel, groups, flips),
        "attend_later",
        [f32(heads, 2 * tokens, HEAD_DIM)] * 3,
        [IN_SMEM] + [IN_VMEM] * (5 + count),
        [IN_VMEM] * 3,
        aliases={3 + count + i: i for i in range(3)},
        flops=8 * heads * tokens * sum(p.shape[0] for p in parts) * HEAD_DIM,
    )(where, *queries, *parts, *running)


def last_kernel(heads, groups, count, flip, where, q_a, q_b, *refs):
    parts, state_refs, outs = refs[:count], refs[count : count + 3], refs[count + 3 :]
    tokens = q_a.shape[0]

    def state(head):
        return tuple(ref[head] for ref in state_refs)

    def store(head, values):
        _, total, mixture = values
        result = (mixture / total).astype(jnp.bfloat16)
        place = (head - heads[0]) * HEAD_DIM
        for side, out in enumerate(outs):
            out[:, place : place + HEAD_DIM] = result[side * tokens : (side + 1) * tokens]

    @pl.when(is_earlier(where, flip))
    def _():
        later_tasks(where[0], heads, groups, q_a, q_b, parts, state, store)

    @pl.when(~is_earlier(where, flip))
    def _():
        for head in heads:
            store(head, state(head))


def attend_last(where, queries, parts, flip, running, heads, groups):
    tokens = queries[0].shape[0]
    count = len(parts)
    return kernel_call(
        functools.partial(last_kernel, heads, groups, count, flip),
        "attend_last",
        [bf16(tokens, len(heads) * HEAD_DIM)] * 2,
        [IN_SMEM] + [IN_VMEM] * (5 + count),
        [IN_VMEM] * 2,
        flops=8 * len(heads) * tokens * sum(p.shape[0] for p in parts) * HEAD_DIM,
    )(where, *queries, *parts, *running)


def place_kernel(places, where, *refs):
    out, sem = refs[-2:]
    half = out.shape[1] // 2
    copies = []
    for part, (received, begin) in zip(refs, places):
        side = 1 - where[0] if received else where[0]
        width = part.shape[1]
        columns = pl.ds(pl.multiple_of(side * half + begin, HEAD_DIM), width)
        copies.append(pltpu.make_async_copy(part, out.at[:, columns], sem.at[len(copies)]))
    run_copies(copies)


def place_heads(where, parts, places, shape, base=None):
    begun = [] if base is None else [base]
    return kernel_call(
        functools.partial(place_kernel, places),
        "place_heads",
        bf16(*shape),
        [IN_SMEM] + [IN_VMEM] * len(parts) + [IN_PLACE] * len(begun),
        IN_PLACE,
        [pltpu.SemaphoreType.DMA((len(parts),))],
        aliases={1 + len(parts): 0} if begun else {},
    )(where, *parts, *begun)


def as_scalars(values):
    return jnp.stack([jnp.asarray(v, jnp.int32) for v in values])


def shards(seq_size, fsdp_size, clean_states, noise_mask, mask_embed, queries, w_key, w_value):
    chips = seq_size // 2
    place = lax.axis_index("seq")
    core = lax.rem(place, 2)
    chip = place // 2
    shard = lax.axis_index("fsdp")
    states = clean_states[0]
    marks = noise_mask
    tokens = states.shape[0]
    depth, kv_width = w_key.shape
    kv_heads = kv_width // 2 // HEAD_DIM

    def swap_cores(array):
        return lax.ppermute(array, "seq", [(s, s ^ 1) for s in range(seq_size)])

    def to_chip(array, flip, sources=None):
        sources = range(chips) if sources is None else sources
        pairs = [(2 * s + c, 2 * (s ^ flip) + c) for s in sources for c in range(2)]
        return lax.ppermute(array, "seq", pairs)

    def to_shard(array, flip):
        return lax.ppermute(array, "fsdp", [(s, s ^ flip) for s in range(fsdp_size)])

    square = chips == CHIPS and fsdp_size == 4
    barrier = lax.optimization_barrier
    where = as_scalars([core, chip, shard])
    query_own = queries[0]
    if square:
        quarter = depth // chips
        half = kv_width // 2
        mine = jnp.concatenate(
            [lax.dynamic_slice(w, (chip * quarter, core * half), (quarter, half)) for w in (w_key, w_value)], 1
        )
        far, near = to_shard(mine, 3), to_shard(mine, 1)

    mask_rows = jnp.broadcast_to(mask_embed[None, :], (MASK_ROWS, mask_embed.shape[0]))
    rows = (states, swap_cores(states), mask_rows)
    query_rows = (query_own, swap_cores(query_own))
    both_marks = (marks, swap_cores(marks))
    steps = jnp.arange(tokens, dtype=jnp.int32)
    cosine, sine = rotation(jnp.concatenate([place * tokens + steps, (place ^ 1) * tokens + steps]))

    if square:
        (corner,) = cut_weights(where, (3,), quarter, w_key, w_value)
        far, near, mine, corner, rows, query_rows, both_marks, cosine, sine = barrier(
            (far, near, mine, corner, rows, query_rows, both_marks, cosine, sine)
        )
        middle = to_shard(mine, 2)
        near_x, far_x = to_chip(near, 1), to_chip(far, 1)
        near_y, far_y = to_chip(near, 2), to_chip(far, 2)
        middle, corner, near_x, near_y, far_x, far_y = barrier((middle, corner, near_x, near_y, far_x, far_y))
        far_corner, near_corner = to_shard(corner, 3), to_shard(corner, 1)
        last = [to_chip(middle, flip) for flip in (3, 1, 2)]
        segments = [
            [((w_key, w_value), 0, None, depth)],
            [
                (far, 3, 0, depth),
                (far_x, 3, 1, depth),
                (far_y, 3, 2, depth),
            ],
            [(near, 1, 0, depth), (near_x, 1, 1, depth), (near_y, 1, 2, depth)],
        ]
        final = [
            [
                (middle, 2, 0, depth),
                (last[0], 2, 3, depth),
                (last[1], 2, 1, depth),
                (last[2], 2, 2, depth),
                (near_corner, 1, 3, depth),
                (far_corner, 3, 3, depth),
            ]
        ]
        staged = project_partial(rows, segments, final, where)
    else:
        (half_weights,) = cut_weights(where, (None,), depth, w_key, w_value)
        gathered = lax.all_gather(half_weights, "fsdp", axis=0, tiled=True)
        final, staged = [[(gathered, None, None, depth)]], ()
    tables = (cosine, sine)
    clean, mask_sums = project_finish(rows, staged, final, where, tables)

    heads = query_own.shape[1] // 2 // HEAD_DIM
    groups = heads // kv_heads
    if square:
        along_x, along_y = to_chip(clean, 1, (0, 1, 2)), to_chip(clean, 2, (0, 1))
        running = attend_own(where, query_rows, tables, both_marks, mask_sums, clean, heads, groups)
        along_x, along_y, running = barrier((along_x, along_y, running))
        last_parts = [to_chip(along_x[:tokens], 2, (0, 1)), to_chip(along_y[tokens:], 1, (2, 3))]
        running = attend_later(where, query_rows, [along_x, along_y], (1, 2), running, groups)
    else:
        running = attend_own(where, query_rows, tables, both_marks, mask_sums, clean, heads, groups)
        for flip in range(1, chips):
            parts = [to_chip(clean, flip, [s for s in range(chips) if s < s ^ flip])]
            if flip < chips - 1:
                running = attend_later(where, query_rows, parts, (flip,), running, groups)
        last_parts = parts
    kept, received = [], []
    middle_head = 3 * heads // 4
    for first, end in ((0, middle_head), (middle_head, heads)):
        own, other = attend_last(
            where, query_rows, last_parts, chips - 1, running, range(first, end), groups
        )
        kept.append(own)
        received.append(swap_cores(other))
    parts = kept + received[:-1]
    begin = middle_head * HEAD_DIM
    places = [(False, 0), (False, begin), (True, 0)]
    output = place_heads(where, parts, places, query_own.shape)
    output = place_heads(where, received[-1:], [(True, begin)], query_own.shape, output)
    return output[None]


def solution(mesh):
    placed = (
        P("fsdp", "seq", None),
        P("fsdp", "seq"),
        P(),
        P("fsdp", "seq", None),
        P("fsdp", None),
        P("fsdp", None),
    )
    return jax.shard_map(
        functools.partial(shards, mesh.shape["seq"], mesh.shape["fsdp"]),
        mesh=mesh,
        in_specs=placed,
        out_specs=P("fsdp", "seq", None),
        check_vma=False,
    )
```
